32 devices in a mesh: fsdp: 4 (over y, x), dp: 8 (over z, core).
Axes of the slice: x: 2, y: 2, z: 4, core: 2. Of those that a mesh axis runs over, the one named last changes fastest.
Arguments:
- noise_embed: bfloat16 [512, 1024], P(('fsdp', 'dp')), may hold values from -6 to 6
- action_embed: bfloat16 [512, 1024], P(('fsdp', 'dp')), may hold values from -6 to 6
- prefix_kv: bfloat16 [2, 32, 256, 256], P(None, ('fsdp', 'dp')), may hold values from -6 to 6
- flow_step: int32 [32], P(('fsdp', 'dp')), may hold values from 0 to 9
- action_mask: int32 [512], P(('fsdp', 'dp')), may hold values 0 or 1
- w_up: bfloat16 [1024, 4096], P(None, 'fsdp'), may hold values from -0.1875 to 0.1875
- w_down: bfloat16 [4096, 1024], P('fsdp'), may hold values from -0.09375 to 0.09375
- query_grad: float32 [1024, 4096], P(None, 'fsdp'), may hold values from -6 to 6
Outputs:
- inverse_hvp: float32 [1024, 4096], P(None, 'fsdp')
- scores: float32 [32], P(('fsdp', 'dp'))
The draws below stay inside these ranges and needn't reach their ends.
All inputs are finite; a program needn't handle non-finite values. No bound on the sum of `action_mask` on one device may be relied on, other than what follows from the above.
Results may differ from the reference program's by a relative error of at most 0.03.
Values may be sent and summed in bfloat16 or wider, within the bound.
A program may use at most 64 MiB of HBM per device.

```python
import math
import jax
import jax.numpy as jnp
from jax import lax

D = 1024
FF = 4096
CHANNEL_SPAN = 256
HEADS = 4
PREFIX = 256
ACT = 16
STEPS_T = 10
ITERS = 2
DEMOS = 32
TOKENS = 512


def place_ends(array, stream_key, smallest, top_value):
    dims = array.shape
    spot = [jax.random.randint(jax.random.fold_in(stream_key, axis), (), 0, dims[axis]) for axis in range(len(dims))]
    array = array.at[tuple(spot)].set(smallest)
    longest = dims.index(max(dims))
    spot[longest] = (spot[longest] + 1) % dims[longest]
    return array.at[tuple(spot)].set(top_value)


def steps_of(key, dims, pieces, smallest, top_value):
    def one(dim, parts):
        draws = jax.random.uniform(jax.random.fold_in(jax.random.fold_in(key, 6), dim), (parts,), jnp.float32, smallest / len(pieces), top_value / len(pieces))
        return jnp.repeat(jnp.exp(draws), dims[dim] // parts).reshape((-1,) + (1,) * (len(dims) - dim - 1))

    loudness = one(*pieces[0])
    for cut in pieces[1:]:
        loudness = loudness * one(*cut)
    return loudness


def bell_draw(key, extent, width, most, shards=(), dtype=jnp.bfloat16):
    values = width * jax.random.normal(key, extent, jnp.float32)
    if shards:
        values = values * steps_of(key, extent, shards, -0.22, 0.18)
    return jnp.clip(values, -most, most).astype(dtype)


def setup_inputs(seed: int = 0) -> dict:
    streams_of = jax.random.split(jax.random.key(seed), 9)
    noise_embed = bell_draw(streams_of[0], (TOKENS, D), 1.0, 6.0, ((0, 32),))
    action_embed = bell_draw(streams_of[1], (TOKENS, D), 1.0, 6.0, ((0, 32),))
    prefix_kv = bell_draw(streams_of[2], (2, DEMOS, PREFIX, CHANNEL_SPAN), 1.0, 6.0, ((1, 32),))
    flow_step = place_ends(jax.random.randint(streams_of[3], (DEMOS,), 0, STEPS_T), jax.random.fold_in(streams_of[3], 1), 0, STEPS_T - 1).astype(jnp.int32)
    action_mask = place_ends((jax.random.randint(streams_of[4], (TOKENS,), 0, 4) < 3).astype(jnp.int32), jax.random.fold_in(streams_of[4], 1), 0, 1)
    w_up = bell_draw(streams_of[5], (D, FF), D ** -0.5, 0.1875, ((1, 4),))
    w_down = bell_draw(streams_of[6], (FF, D), FF ** -0.5, 0.09375, ((0, 4),))
    query_grad = bell_draw(streams_of[7], (D, FF), 1.0, 6.0, ((1, 4),), jnp.float32)
    return dict(noise_embed=noise_embed, action_embed=action_embed, prefix_kv=prefix_kv, flow_step=flow_step, action_mask=action_mask, w_up=w_up, w_down=w_down, query_grad=query_grad)


epsilon = 1e-06
sharpness_divisor = 6.0
damping_factor = 0.01

def attend(noise_embed, action_embed, prefix_kv, flow_step):
    demos = flow_step.shape[0]
    times = (flow_step.astype(jnp.float32) + 1.0) / (STEPS_T + 1.0)
    per_token = jnp.repeat(times, ACT)[:, None]
    noisy = noise_embed.astype(jnp.float32)
    clean = action_embed.astype(jnp.float32)
    inputs = per_token * noisy + (1.0 - per_token) * clean
    target = noisy - clean
    queries = inputs.reshape(demos, ACT, HEADS, CHANNEL_SPAN)
    probe_length = (queries * lax.rsqrt(lax.optimization_barrier(jnp.mean(queries * queries, -1, keepdims=True)) + epsilon)).astype(jnp.bfloat16)
    keys = prefix_kv[0].astype(jnp.float32)
    lookup_length = (keys * lax.rsqrt(lax.optimization_barrier(jnp.mean(keys * keys, -1, keepdims=True)) + epsilon)).astype(jnp.bfloat16)
    match_energies = jnp.einsum('zilf,zgf->zilg', probe_length.astype(jnp.float32), lookup_length.astype(jnp.float32)) * (sharpness_divisor / CHANNEL_SPAN)
    expo = jnp.exp(match_energies)
    weights = (expo / lax.optimization_barrier(jnp.sum(expo, -1, keepdims=True))).astype(jnp.bfloat16)
    mixed = jnp.einsum('dahp,dpe->dahe', weights.astype(jnp.float32), prefix_kv[1].astype(jnp.float32))
    hidden = inputs + mixed.reshape(demos * ACT, HEADS * CHANNEL_SPAN)
    normed_rows = (hidden * lax.rsqrt(lax.optimization_barrier(jnp.mean(hidden * hidden, -1, keepdims=True)) + epsilon)).astype(jnp.bfloat16)
    return (hidden, normed_rows, target)

def reference(noise_embed, action_embed, prefix_kv, flow_step, action_mask, w_up, w_down, query_grad):
    hidden, normed_rows, target = attend(noise_embed, action_embed, prefix_kv, flow_step)
    pre = jnp.dot(normed_rows, w_up, preferred_element_type=jnp.float32)
    sig = jax.nn.sigmoid(pre)
    slopes = sig * (1.0 + pre * (1.0 - sig))
    curves = sig * (1.0 - sig) * (2.0 + pre * (1.0 - 2.0 * sig))
    active = (pre * sig).astype(jnp.bfloat16)
    output = jnp.dot(active, w_down, preferred_element_type=jnp.float32)
    mask = action_mask.astype(jnp.float32)[:, None]
    err = (mask * (hidden + output - target)).astype(jnp.bfloat16)
    pulled = jnp.dot(err, w_down.T, preferred_element_type=jnp.float32)
    back = pulled * slopes

    def curvature(vector):
        direction_vector = jnp.dot(normed_rows, vector.astype(jnp.bfloat16), preferred_element_type=jnp.float32)
        linear = (slopes * direction_vector).astype(jnp.bfloat16)
        moved = jnp.dot(linear, w_down, preferred_element_type=jnp.float32)
        moved_err = (mask * moved).astype(jnp.bfloat16)
        second = (jnp.dot(moved_err, w_down.T, preferred_element_type=jnp.float32) * slopes + pulled * curves * direction_vector).astype(jnp.bfloat16)
        aggregate_total = lax.dot_general(normed_rows, second, (((0,), (0,)), ((), ())), preferred_element_type=jnp.float32)
        return aggregate_total / TOKENS
    vector = query_grad
    for step in range(ITERS):
        vector = query_grad + (1.0 - damping_factor) * vector - curvature(vector)
    projected = jnp.dot(normed_rows, vector.astype(jnp.bfloat16), preferred_element_type=jnp.float32)
    token_terms = lax.optimization_barrier(jnp.sum(projected * back, -1))
    scores = -lax.optimization_barrier(jnp.sum(token_terms.reshape(-1, ACT), -1)) / (ACT * math.sqrt(D * FF))
    return (vector, scores)
```

```python
import math

import jax
import jax.numpy as jnp
from jax import lax
from jax.sharding import PartitionSpec as P

STEPS_T = 10

epsilon = 1e-06
sharpness_divisor = 6.0
keep = 1.0 - 0.01


def attend(noise_embed, action_embed, prefix_kv, flow_step):
    demos = flow_step.shape[0]
    acts = noise_embed.shape[0] // demos
    channel_span = prefix_kv.shape[3]
    width = noise_embed.shape[1]
    times = (flow_step.astype(jnp.float32) + 1.0) / (STEPS_T + 1.0)
    per_token = jnp.repeat(times, acts)[:, None]
    noisy = noise_embed.astype(jnp.float32)
    clean = action_embed.astype(jnp.float32)
    inputs = per_token * noisy + (1.0 - per_token) * clean
    target = noisy - clean
    queries = inputs.reshape(demos, acts, width // channel_span, channel_span)
    probe_length = (
        queries * lax.rsqrt(jnp.mean(queries * queries, -1, keepdims=True) + epsilon)
    ).astype(jnp.bfloat16)
    keys = prefix_kv[0].astype(jnp.float32)
    lookup_length = (keys * lax.rsqrt(jnp.mean(keys * keys, -1, keepdims=True) + epsilon)).astype(
        jnp.bfloat16
    )
    match_energies = jnp.einsum(
        "zilf,zgf->zilg", probe_length, lookup_length, preferred_element_type=jnp.float32
    ) * (sharpness_divisor / channel_span)
    expo = jnp.exp(match_energies)
    weights = (expo / jnp.sum(expo, -1, keepdims=True)).astype(jnp.bfloat16)
    mixed = jnp.einsum("dahp,dpe->dahe", weights, prefix_kv[1], preferred_element_type=jnp.float32)
    hidden = inputs + mixed.reshape(demos * acts, width)
    normed_rows = (
        hidden * lax.rsqrt(jnp.mean(hidden * hidden, -1, keepdims=True) + epsilon)
    ).astype(jnp.bfloat16)
    return (hidden, normed_rows, target, acts)


def dot32(a, b):
    return jnp.dot(a, b, preferred_element_type=jnp.float32)


def shards(noise_embed, action_embed, prefix_kv, flow_step, action_mask, w_up, w_down, query_grad):
    hidden, normed_rows, target, acts = attend(noise_embed, action_embed, prefix_kv, flow_step)
    tok_rows, width = normed_rows.shape
    nf = lax.axis_size("fsdp")
    mask_own = action_mask.astype(jnp.float32)[:, None]
    gathered = lax.all_gather(normed_rows, "fsdp", axis=0, tiled=True)
    every = lax.all_gather(gathered, "dp", axis=0, tiled=True)
    rows = gathered.shape[0]
    total = tok_rows * nf * lax.axis_size("dp")
    pre = dot32(gathered, w_up)
    sig = jax.nn.sigmoid(pre)
    slopes = sig * (1.0 + pre * (1.0 - sig))
    curves = sig * (1.0 - sig) * (2.0 + pre * (1.0 - 2.0 * sig))
    active = (pre * sig).astype(jnp.bfloat16)
    tangent0 = dot32(gathered, query_grad.astype(jnp.bfloat16))
    linear = (slopes * tangent0).astype(jnp.bfloat16)
    both = jnp.concatenate(
        [dot32(active, w_down).astype(jnp.bfloat16), dot32(linear, w_down).astype(jnp.bfloat16)], 1
    )
    both = lax.psum_scatter(both, "fsdp", scatter_dimension=0, tiled=True).astype(jnp.float32)
    err = mask_own * (hidden + both[:, :width] - target)
    moved_err = mask_own * both[:, width:]
    pair = jnp.concatenate([err, moved_err], 1).astype(jnp.bfloat16)
    pair = lax.all_gather(pair, "fsdp", axis=0, tiled=True)
    pulled = dot32(pair[:, :width], w_down.T)
    back = pulled * slopes
    bent = pulled * curves
    second = (dot32(pair[:, width:], w_down.T) * slopes + bent * tangent0).astype(jnp.bfloat16)
    seconds0 = lax.all_gather(second, "dp", axis=0, tiled=True)
    gram = (lax.dot_general(gathered, every, (((1,), (1,)), ((), ())), preferred_element_type=jnp.float32) / total).astype(jnp.bfloat16)
    tangent1 = (1.0 + keep) * tangent0 - dot32(gram, seconds0)
    linear = (slopes * tangent1).astype(jnp.bfloat16)
    moved = lax.psum_scatter(
        dot32(linear, w_down).astype(jnp.bfloat16), "fsdp", scatter_dimension=0, tiled=True
    ).astype(jnp.float32)
    moved_all = lax.all_gather((mask_own * moved).astype(jnp.bfloat16), "fsdp", axis=0, tiled=True)
    second = (dot32(moved_all, w_down.T) * slopes + bent * tangent1).astype(jnp.bfloat16)
    seconds1 = lax.all_gather(second, "dp", axis=0, tiled=True)
    mix = (keep * seconds0.astype(jnp.float32) + seconds1.astype(jnp.float32)).astype(jnp.bfloat16)
    change = lax.dot_general(every, mix, (((0,), (0,)), ((), ())), preferred_element_type=jnp.float32) / total
    scale = 1.0 + keep + keep * keep
    vector = scale * query_grad - change
    projected = scale * tangent0 - dot32(gram, mix)
    token_terms = jnp.sum(projected * back, -1)
    demo_terms = jnp.sum(token_terms.reshape(-1, acts), -1)
    owned = lax.psum_scatter(demo_terms, "fsdp", scatter_dimension=0, tiled=True)
    return (vector, -owned / (acts * math.sqrt(query_grad.shape[0] * query_grad.shape[1] * nf)))


def solution(mesh):
    placed = (
        P(("fsdp", "dp"), None),
        P(("fsdp", "dp"), None),
        P(None, ("fsdp", "dp"), None, None),
        P(("fsdp", "dp")),
        P(("fsdp", "dp")),
        P(None, "fsdp"),
        P("fsdp", None),
        P(None, "fsdp"),
    )
    return jax.shard_map(
        shards,
        mesh=mesh,
        in_specs=placed,
        out_specs=(P(None, "fsdp"), P(("fsdp", "dp"))),
        check_vma=False,
    )
```

```python
import functools
import math

import jax
import jax.numpy as jnp
from jax import lax
from jax.experimental import pallas as pl
from jax.experimental.pallas import tpu as pltpu
from jax.sharding import PartitionSpec as P

STEPS_T = 10
CORES = 2

epsilon = 1e-06
sharpness_divisor = 6.0
keep = 1.0 - 0.01

BF = jnp.bfloat16
F32 = jnp.float32
MESH = pl.DeviceIdType.MESH


def dot32(a, b):
    return jnp.dot(a, b, preferred_element_type=F32)


def dot_t(a, b):
    return lax.dot_general(a, b, (((1,), (1,)), ((), ())), preferred_element_type=F32)


def loop(count, body):
    if count == 1:
        body(0)
    else:
        pl.loop(0, count)(body)


def tile(i, size):
    return pl.ds(pl.multiple_of(i * size, size), size)


def attend(noise, action, kv, flow):
    acts, width = noise.shape
    span = kv.shape[3]
    heads = width // span
    time = (flow[0].astype(F32) + 1.0) / (STEPS_T + 1.0)
    noisy = noise[...].astype(F32)
    clean = action[...].astype(F32)
    inputs = time * noisy + (1.0 - time) * clean
    queries = jnp.concatenate([inputs[:, h * span : (h + 1) * span] for h in range(heads)], 0)
    queries = queries * lax.rsqrt(jnp.mean(queries * queries, -1, keepdims=True) + epsilon)
    keys = kv[0, 0].astype(F32)
    keys = keys * lax.rsqrt(jnp.mean(keys * keys, -1, keepdims=True) + epsilon)
    expo = jnp.exp(dot_t(queries.astype(BF), keys.astype(BF)) * (sharpness_divisor / span))
    weights = (expo / jnp.sum(expo, -1, keepdims=True)).astype(BF)
    mixed = dot32(weights, kv[1, 0])
    mixed = jnp.concatenate([mixed[h * acts : (h + 1) * acts] for h in range(heads)], 1)
    hidden = inputs + mixed
    normed = hidden * lax.rsqrt(jnp.mean(hidden * hidden, -1, keepdims=True) + epsilon)
    return normed.astype(BF), hidden - (noisy - clean)


def kernel(
    nf, nd,
    noise, action, kv, flow, mask, w_up_h, w_down_h, grad_h,
    every_o, mix_o, score,
    w_up, w_down, grad, every, seconds0, seconds1, gram,
    slopes, curves, pulled, tan0, tan1, lhs, part, land0, land1, pair0, pair1,
    resid, tally, tally_in,
    load_sem, store_sem, f_send, f_recv, z_send, z_recv, c_send, c_recv,
):
    acts, width = noise.shape
    hid = w_up.shape[1]
    rows = nf * acts
    total = nd * rows
    chips = nd // CORES
    f = lax.axis_index("fsdp")
    d = lax.axis_index("dp")
    chip, core = d // CORES, d % CORES
    sibling = chip * CORES + (1 - core)

    def f_peer(k):
        return lax.rem(f + k, nf)

    def d_peer(k):
        return lax.rem(chip + k, chips) * CORES + core

    def d_from(k):
        return lax.rem(chip + chips - k, chips) * CORES + core

    barrier = pltpu.get_barrier_semaphore()
    for k in range(1, nf):
        pl.semaphore_signal(barrier, inc=1, device_id=(f_peer(k), d), device_id_type=MESH)
    for k in range(1, chips):
        pl.semaphore_signal(barrier, inc=1, device_id=(f, d_peer(k)), device_id_type=MESH)
    pl.semaphore_signal(barrier, inc=1, device_id=(f, sibling), device_id_type=MESH)

    loads = [
        pltpu.make_async_copy(src, dst, load_sem.at[i])
        for i, (src, dst) in enumerate(((w_up_h, w_up), (grad_h, grad), (w_down_h, w_down)))
    ]
    for load in loads:
        load.start()

    def remote(src, dst, send, recv, who):
        copy = pltpu.make_async_remote_copy(
            src_ref=src, dst_ref=dst, send_sem=send, recv_sem=recv, device_id=who, device_id_type=MESH
        )
        copy.start()
        return copy

    sent = []

    def fsdp(phase, src, dst):
        copies = [
            remote(src(f_peer(k)), dst(k), f_send.at[phase, k], f_recv.at[phase, k], (f_peer(k), d))
            for k in range(1, nf)
        ]
        if phase not in (1, 2):
            sent.extend(copies)
        return copies

    def landed(copies):
        for copy in copies:
            copy.wait_recv()

    def dp_start(phase, buf):
        mine = buf.at[tile(d, rows), :]
        z = [
            remote(mine, mine, z_send.at[phase, k], z_recv.at[phase, k], (f, d_peer(k)))
            for k in range(1, chips)
        ]
        c = [remote(mine, mine, c_send.at[phase, 0], c_recv.at[phase, 0], (f, sibling))]
        sent.extend(z)
        sent.extend(c)
        return z, c

    def dp_forward(phase, buf, z, c):
        for k in range(1, chips):
            z[k - 1].wait_recv()
            block = buf.at[tile(d_from(k), rows), :]
            copy = remote(block, block, c_send.at[phase, k], c_recv.at[phase, k], (f, sibling))
            sent.append(copy)
            c.append(copy)

    normed, left = attend(noise, action, kv, flow)
    resid[...] = left
    own = pl.ds(pl.multiple_of(d * rows + f * acts, acts), acts)
    every[own, :] = normed
    lane = lax.broadcasted_iota(jnp.int32, (acts, acts), 1)
    line = lax.broadcasted_iota(jnp.int32, (acts, acts), 0)
    valid = jnp.sum(
        jnp.where(lane == line, jnp.broadcast_to(mask[...].astype(F32), (acts, acts)), 0.0), -1, keepdims=True
    )
    pl.semaphore_wait(barrier, nf - 1 + chips)

    mine = every.at[own, :]
    landed(fsdp(0, lambda p: mine, lambda k: mine))
    group_at = tile(d, rows)
    z_n, c_n = dp_start(0, every)

    loads[0].wait()
    loads[1].wait()
    step = min(256, hid)

    def first(i):
        cut = tile(i, step)
        group = every[group_at, :]
        pre = dot32(group, w_up[:, cut])
        tangent = dot32(group, grad[:, cut].astype(BF))
        sig = 1.0 / (1.0 + jnp.exp(-pre))
        slope = sig * (1.0 + pre * (1.0 - sig))
        slopes[:, cut] = slope
        curves[:, cut] = sig * (1.0 - sig) * (2.0 + pre * (1.0 - 2.0 * sig))
        tan0[:, cut] = tangent
        lhs[0:rows, cut] = (pre * sig).astype(BF)
        lhs[rows : 2 * rows, cut] = (slope * tangent).astype(BF)

    loop(hid // step, first)
    loads[2].wait()
    wide = min(256, width)

    def down(i):
        cut = tile(i, wide)
        part[:, cut] = dot32(lhs[...], w_down[:, cut]).astype(BF)

    loop(width // wide, down)

    def rows_of(p, q):
        return pl.ds(pl.multiple_of(q * rows + p * acts, acts), acts)

    outs = fsdp(1, lambda p: part.at[rows_of(p, 0), :], lambda k: land0.at[k, 0:acts, :])
    moves = fsdp(2, lambda p: part.at[rows_of(p, 1), :], lambda k: land0.at[k, acts : 2 * acts, :])

    def summed(copies, q, land, lo):
        value = part[rows_of(f, q), :].astype(F32)
        for k in range(1, nf):
            copies[k - 1].wait_recv()
            value = value + land[k, lo : lo + acts, :].astype(F32)
        return value

    err = (valid * (resid[...] + summed(outs, 0, land0, 0))).astype(BF)
    pair0[rows_of(f, 0), :] = err
    errs = fsdp(3, lambda p: pair0.at[rows_of(f, 0), :], lambda k: pair0.at[rows_of(f, 0), :])
    pair0[rows_of(f, 1), :] = (valid * summed(moves, 1, land0, acts)).astype(BF)
    merrs = fsdp(4, lambda p: pair0.at[rows_of(f, 1), :], lambda k: pair0.at[rows_of(f, 1), :])
    dp_forward(0, every, z_n, c_n)
    landed(errs)
    landed(merrs)

    def bend(i):
        cut = tile(i, step)
        both = dot_t(pair0[...], w_down[cut, :])
        pull = both[0:rows]
        pulled[:, cut] = pull
        seconds0[group_at, cut] = (
            both[rows : 2 * rows] * slopes[:, cut] + pull * curves[:, cut] * tan0[:, cut]
        ).astype(BF)

    loop(hid // step, bend)
    z_0, c_0 = dp_start(1, seconds0)
    landed(c_n)
    keep_every = pltpu.make_async_copy(every, every_o, store_sem.at[0])
    keep_every.start()
    chunk = min(512, total)

    def grams(i):
        cut = tile(i, chunk)
        gram[:, cut] = (dot_t(every[group_at, :], every[cut, :]) / total).astype(BF)

    loop(total // chunk, grams)
    dp_forward(1, seconds0, z_0, c_0)
    landed(c_0)

    def fold(seconds, cut):
        if total == chunk:
            return dot32(gram[...], seconds[:, cut])
        return lax.fori_loop(
            0,
            total // chunk,
            lambda j, v: v + dot32(gram[:, tile(j, chunk)], seconds[tile(j, chunk), cut]),
            jnp.zeros((rows, step), F32),
        )

    def again(i):
        cut = tile(i, step)
        tangent = (1.0 + keep) * tan0[:, cut] - fold(seconds0, cut)
        tan1[:, cut] = tangent
        lhs[0:rows, cut] = (slopes[:, cut] * tangent).astype(BF)

    loop(hid // step, again)
    for copy in outs + moves:
        copy.wait_send()

    def down_again(i):
        cut = tile(i, wide)
        part[0:rows, cut] = dot32(lhs[0:rows, :], w_down[:, cut]).astype(BF)

    loop(width // wide, down_again)
    moves1 = fsdp(5, lambda p: part.at[rows_of(p, 0), :], lambda k: land1.at[k])
    pair1[rows_of(f, 0), :] = (valid * summed(moves1, 0, land1, 0)).astype(BF)
    landed(fsdp(6, lambda p: pair1.at[rows_of(f, 0), :], lambda k: pair1.at[rows_of(f, 0), :]))

    def bend_again(i):
        cut = tile(i, step)
        both = dot_t(pair1[...], w_down[cut, :])
        seconds1[group_at, cut] = (
            both * slopes[:, cut] + pulled[:, cut] * curves[:, cut] * tan1[:, cut]
        ).astype(BF)

    loop(hid // step, bend_again)
    z_1, c_1 = dp_start(2, seconds1)
    dp_forward(2, seconds1, z_1, c_1)
    landed(c_1)
    for copy in sent:
        copy.wait_send()

    def blend(i):
        cut = tile(i, rows)
        seconds1[cut, :] = (
            keep * seconds0[cut, :].astype(F32) + seconds1[cut, :].astype(F32)
        ).astype(BF)

    loop(nd, blend)
    keep_mix = pltpu.make_async_copy(seconds1, mix_o, store_sem.at[1])
    keep_mix.start()
    scale = 1.0 + keep + keep * keep

    def rate(i, terms):
        cut = tile(i, step)
        projected = scale * tan0[:, cut] - fold(seconds1, cut)
        return terms + projected * (pulled[:, cut] * slopes[:, cut])

    terms = lax.fori_loop(0, hid // step, rate, jnp.zeros((rows, step), F32))
    for p in range(nf):
        one = jnp.sum(terms[p * acts : (p + 1) * acts], 0, keepdims=True)
        tally[p] = jnp.broadcast_to(jnp.sum(one, -1, keepdims=True), tally.shape[1:])
    votes = [
        remote(tally.at[f_peer(k)], tally_in.at[k], f_send.at[7, k], f_recv.at[7, k], (f_peer(k), d))
        for k in range(1, nf)
    ]
    value = tally[f]
    for k in range(1, nf):
        votes[k - 1].wait_recv()
        value = value + tally_in[k]
    score[...] = -value / (acts * math.sqrt(width * hid * nf))
    for copy in votes:
        copy.wait_send()
    keep_every.wait()
    keep_mix.wait()


def finish(total, every, mix, grad, out):
    change = lax.dot_general(
        every[...], mix[...], (((0,), (0,)), ((), ())), preferred_element_type=F32
    )
    out[...] = (1.0 + keep + keep * keep) * grad[...] - change / total


def shards(nf, nd, noise, action, kv, flow, mask, w_up, w_down, grad):
    acts, width = noise.shape
    hid = w_up.shape[1]
    rows = nf * acts
    total = nd * rows
    vmem = pl.BlockSpec(memory_space=pltpu.VMEM)
    anywhere = pl.BlockSpec(memory_space=pl.ANY)
    dma = pltpu.SemaphoreType.DMA
    chips = nd // CORES
    every, mix, score = pl.pallas_call(
        functools.partial(kernel, nf, nd),
        out_shape=(
            jax.ShapeDtypeStruct((total, width), BF),
            jax.ShapeDtypeStruct((total, hid), BF),
            jax.ShapeDtypeStruct((8, 128), F32),
        ),
        in_specs=[
            vmem, vmem, vmem, pl.BlockSpec(memory_space=pltpu.SMEM), vmem, anywhere, anywhere, anywhere,
        ],
        out_specs=(anywhere, anywhere, vmem),
        scratch_shapes=[
            pltpu.VMEM((width, hid), BF),
            pltpu.VMEM((hid, width), BF),
            pltpu.VMEM((width, hid), F32),
            pltpu.VMEM((total, width), BF),
            pltpu.VMEM((total, hid), BF),
            pltpu.VMEM((total, hid), BF),
            pltpu.VMEM((rows, total), BF),
            pltpu.VMEM((rows, hid), F32),
            pltpu.VMEM((rows, hid), F32),
            pltpu.VMEM((rows, hid), F32),
            pltpu.VMEM((rows, hid), F32),
            pltpu.VMEM((rows, hid), F32),
            pltpu.VMEM((2 * rows, hid), BF),
            pltpu.VMEM((2 * rows, width), BF),
            pltpu.VMEM((nf, 2 * acts, width), BF),
            pltpu.VMEM((nf, acts, width), BF),
            pltpu.VMEM((2 * rows, width), BF),
            pltpu.VMEM((rows, width), BF),
            pltpu.VMEM((acts, width), F32),
            pltpu.VMEM((nf, 8, 128), F32),
            pltpu.VMEM((nf, 8, 128), F32),
            dma((3,)),
            dma((2,)),
            dma((8, nf)),
            dma((8, nf)),
            dma((3, chips)),
            dma((3, chips)),
            dma((3, chips)),
            dma((3, chips)),
        ],
        compiler_params=pltpu.CompilerParams(
            collective_id=0, has_side_effects=True, vmem_limit_bytes=52 * 1024 * 1024
        ),
        name="lissa",
    )(noise, action, kv, flow, mask.reshape(1, acts), w_up, w_down, grad)
    strip = 128
    vector = pl.pallas_call(
        functools.partial(finish, total),
        out_shape=jax.ShapeDtypeStruct((width, hid), F32),
        grid=(width // strip,),
        in_specs=[
            pl.BlockSpec((total, strip), lambda i: (0, i)),
            pl.BlockSpec((total, hid), lambda i: (0, 0)),
            pl.BlockSpec((strip, hid), lambda i: (i, 0)),
        ],
        out_specs=pl.BlockSpec((strip, hid), lambda i: (i, 0)),
        compiler_params=pltpu.CompilerParams(vmem_limit_bytes=40 * 1024 * 1024),
        name="finish",
    )(every, mix, grad)
    return vector, score[0, 0:1]


def solution(mesh):
    placed = (
        P(("fsdp", "dp"), None),
        P(("fsdp", "dp"), None),
        P(None, ("fsdp", "dp"), None, None),
        P(("fsdp", "dp")),
        P(("fsdp", "dp")),
        P(None, "fsdp"),
        P("fsdp", None),
        P(None, "fsdp"),
    )
    return jax.shard_map(
        functools.partial(shards, mesh.shape["fsdp"], mesh.shape["dp"]),
        mesh=mesh,
        in_specs=placed,
        out_specs=(P(None, "fsdp"), P(("fsdp", "dp"))),
        check_vma=False,
    )
```

```python
import functools
import math

import jax
import jax.numpy as jnp
from jax import lax
from jax.experimental import pallas as pl
from jax.experimental.pallas import tpu as pltpu
from jax.sharding import PartitionSpec as P

STEPS_T = 10
CORES = 2

epsilon = 1e-06
sharpness_divisor = 6.0
keep = 1.0 - 0.01

BF = jnp.bfloat16
F32 = jnp.float32
MESH = pl.DeviceIdType.MESH


def dot32(a, b):
    return jnp.dot(a, b, preferred_element_type=F32)


def dot_t(a, b):
    return lax.dot_general(a, b, (((1,), (1,)), ((), ())), preferred_element_type=F32)


def loop(count, body):
    if count == 1:
        body(0)
    else:
        pl.loop(0, count)(body)


def tile(i, size):
    return pl.ds(pl.multiple_of(i * size, size), size)


def attend(noise, action, kv, flow):
    acts, width = noise.shape
    span = kv.shape[3]
    heads = width // span
    time = (flow[0].astype(F32) + 1.0) / (STEPS_T + 1.0)
    noisy = noise[...].astype(F32)
    clean = action[...].astype(F32)
    inputs = time * noisy + (1.0 - time) * clean
    queries = jnp.concatenate([inputs[:, h * span : (h + 1) * span] for h in range(heads)], 0)
    queries = queries * lax.rsqrt(jnp.mean(queries * queries, -1, keepdims=True) + epsilon)
    keys = kv[0, 0].astype(F32)
    keys = keys * lax.rsqrt(jnp.mean(keys * keys, -1, keepdims=True) + epsilon)
    expo = jnp.exp(dot_t(queries.astype(BF), keys.astype(BF)) * (sharpness_divisor / span))
    weights = (expo / jnp.sum(expo, -1, keepdims=True)).astype(BF)
    mixed = dot32(weights, kv[1, 0])
    mixed = jnp.concatenate([mixed[h * acts : (h + 1) * acts] for h in range(heads)], 1)
    hidden = inputs + mixed
    normed = hidden * lax.rsqrt(jnp.mean(hidden * hidden, -1, keepdims=True) + epsilon)
    return normed.astype(BF), hidden - (noisy - clean)


def kernel(
    nf, nd,
    noise, action, kv, flow, mask, w_up_h, w_down_h, grad_h,
    every_o, mix_o, score,
    w_up, w_down, grad, every, seconds0, seconds1, gram,
    slopes, curves, pulled, tan0, tan1, lhs, part, land0, land1, pair0, pair1,
    resid, tally, tally_in,
    load_sem, store_sem, f_send, f_recv, z_send, z_recv, c_send, c_recv,
):
    acts, width = noise.shape
    hid = w_up.shape[1]
    rows = nf * acts
    total = nd * rows
    chips = nd // CORES
    f = lax.axis_index("fsdp")
    d = lax.axis_index("dp")
    chip, core = d // CORES, d % CORES
    sibling = chip * CORES + (1 - core)

    def f_peer(k):
        return lax.rem(f + k, nf)

    def d_peer(k):
        return lax.rem(chip + k, chips) * CORES + core

    def d_from(k):
        return lax.rem(chip + chips - k, chips) * CORES + core

    barrier = pltpu.get_barrier_semaphore()
    for k in range(1, nf):
        pl.semaphore_signal(barrier, inc=1, device_id=(f_peer(k), d), device_id_type=MESH)
    for k in range(1, chips):
        pl.semaphore_signal(barrier, inc=1, device_id=(f, d_peer(k)), device_id_type=MESH)
    pl.semaphore_signal(barrier, inc=1, device_id=(f, sibling), device_id_type=MESH)

    loads = [
        pltpu.make_async_copy(src, dst, load_sem.at[i])
        for i, (src, dst) in enumerate(((w_up_h, w_up), (grad_h, grad), (w_down_h, w_down)))
    ]
    for load in loads:
        load.start()

    def remote(src, dst, send, recv, who):
        copy = pltpu.make_async_remote_copy(
            src_ref=src, dst_ref=dst, send_sem=send, recv_sem=recv, device_id=who, device_id_type=MESH
        )
        copy.start()
        return copy

    sent = []

    def fsdp(phase, src, dst):
        copies = [
            remote(src(f_peer(k)), dst(k), f_send.at[phase, k], f_recv.at[phase, k], (f_peer(k), d))
            for k in range(1, nf)
        ]
        if phase not in (1, 2):
            sent.extend(copies)
        return copies

    def landed(copies):
        for copy in copies:
            copy.wait_recv()

    def dp_start(phase, buf):
        mine = buf.at[tile(d, rows), :]
        z = [
            remote(mine, mine, z_send.at[phase, k], z_recv.at[phase, k], (f, d_peer(k)))
            for k in range(1, chips)
        ]
        c = [remote(mine, mine, c_send.at[phase, 0], c_recv.at[phase, 0], (f, sibling))]
        sent.extend(z)
        sent.extend(c)
        return z, c

    def dp_forward(phase, buf, z, c):
        for k in range(1, chips):
            z[k - 1].wait_recv()
            block = buf.at[tile(d_from(k), rows), :]
            copy = remote(block, block, c_send.at[phase, k], c_recv.at[phase, k], (f, sibling))
            sent.append(copy)
            c.append(copy)

    normed, left = attend(noise, action, kv, flow)
    resid[...] = left
    own = pl.ds(pl.multiple_of(d * rows + f * acts, acts), acts)
    every[own, :] = normed
    lane = lax.broadcasted_iota(jnp.int32, (acts, acts), 1)
    line = lax.broadcasted_iota(jnp.int32, (acts, acts), 0)
    valid = jnp.sum(
        jnp.where(lane == line, jnp.broadcast_to(mask[...].astype(F32), (acts, acts)), 0.0), -1, keepdims=True
    )
    pl.semaphore_wait(barrier, nf - 1 + chips)

    mine = every.at[own, :]
    landed(fsdp(0, lambda p: mine, lambda k: mine))
    group_at = tile(d, rows)
    z_n, c_n = dp_start(0, every)

    loads[0].wait()
    loads[1].wait()
    step = min(256, hid)

    def first(i):
        cut = tile(i, step)
        group = every[group_at, :]
        pre = dot32(group, w_up[:, cut])
        tangent = dot32(group, grad[:, cut].astype(BF))
        sig = 1.0 / (1.0 + jnp.exp(-pre))
        slope = sig * (1.0 + pre * (1.0 - sig))
        slopes[:, cut] = slope
        curves[:, cut] = sig * (1.0 - sig) * (2.0 + pre * (1.0 - 2.0 * sig))
        tan0[:, cut] = tangent
        lhs[0:rows, cut] = (pre * sig).astype(BF)
        lhs[rows : 2 * rows, cut] = (slope * tangent).astype(BF)

    loop(hid // step, first)
    loads[2].wait()
    wide = min(256, width)

    def down(i):
        cut = tile(i, wide)
        part[:, cut] = dot32(lhs[...], w_down[:, cut]).astype(BF)

    loop(width // wide, down)

    def rows_of(p, q):
        return pl.ds(pl.multiple_of(q * rows + p * acts, acts), acts)

    outs = fsdp(1, lambda p: part.at[rows_of(p, 0), :], lambda k: land0.at[k, 0:acts, :])
    moves = fsdp(2, lambda p: part.at[rows_of(p, 1), :], lambda k: land0.at[k, acts : 2 * acts, :])

    def summed(copies, q, land, lo):
        value = part[rows_of(f, q), :].astype(F32)
        for k in range(1, nf):
            copies[k - 1].wait_recv()
            value = value + land[k, lo : lo + acts, :].astype(F32)
        return value

    err = (valid * (resid[...] + summed(outs, 0, land0, 0))).astype(BF)
    pair0[rows_of(f, 0), :] = err
    errs = fsdp(3, lambda p: pair0.at[rows_of(f, 0), :], lambda k: pair0.at[rows_of(f, 0), :])
    pair0[rows_of(f, 1), :] = (valid * summed(moves, 1, land0, acts)).astype(BF)
    merrs = fsdp(4, lambda p: pair0.at[rows_of(f, 1), :], lambda k: pair0.at[rows_of(f, 1), :])
    dp_forward(0, every, z_n, c_n)
    landed(errs)
    landed(merrs)

    def bend(i):
        cut = tile(i, step)
        both = dot_t(pair0[...], w_down[cut, :])
        pull = both[0:rows]
        pulled[:, cut] = pull
        seconds0[group_at, cut] = (
            both[rows : 2 * rows] * slopes[:, cut] + pull * curves[:, cut] * tan0[:, cut]
        ).astype(BF)

    loop(hid // step, bend)
    z_0, c_0 = dp_start(1, seconds0)
    landed(c_n)
    keep_every = pltpu.make_async_copy(every, every_o, store_sem.at[0])
    keep_every.start()
    chunk = min(512, total)

    def grams(i):
        cut = tile(i, chunk)
        gram[:, cut] = (dot_t(every[group_at, :], every[cut, :]) / total).astype(BF)

    loop(total // chunk, grams)
    dp_forward(1, seconds0, z_0, c_0)
    landed(c_0)

    def fold(seconds, cut):
        if total == chunk:
            return dot32(gram[...], seconds[:, cut])
        return lax.fori_loop(
            0,
            total // chunk,
            lambda j, v: v + dot32(gram[:, tile(j, chunk)], seconds[tile(j, chunk), cut]),
            jnp.zeros((rows, step), F32),
        )

    def again(i):
        cut = tile(i, step)
        tangent = (1.0 + keep) * tan0[:, cut] - fold(seconds0, cut)
        tan1[:, cut] = tangent
        lhs[0:rows, cut] = (slopes[:, cut] * tangent).astype(BF)

    loop(hid // step, again)
    for copy in outs + moves:
        copy.wait_send()

    def down_again(i):
        cut = tile(i, wide)
        part[0:rows, cut] = dot32(lhs[0:rows, :], w_down[:, cut]).astype(BF)

    loop(width // wide, down_again)
    moves1 = fsdp(5, lambda p: part.at[rows_of(p, 0), :], lambda k: land1.at[k])
    pair1[rows_of(f, 0), :] = (valid * summed(moves1, 0, land1, 0)).astype(BF)
    landed(fsdp(6, lambda p: pair1.at[rows_of(f, 0), :], lambda k: pair1.at[rows_of(f, 0), :]))

    def bend_again(i):
        cut = tile(i, step)
        both = dot_t(pair1[...], w_down[cut, :])
        seconds1[group_at, cut] = (
            both * slopes[:, cut] + pulled[:, cut] * curves[:, cut] * tan1[:, cut]
        ).astype(BF)

    loop(hid // step, bend_again)
    z_1, c_1 = dp_start(2, seconds1)
    dp_forward(2, seconds1, z_1, c_1)
    landed(c_1)
    for copy in sent:
        copy.wait_send()

    def blend(i):
        cut = tile(i, rows)
        seconds1[cut, :] = (
            keep * seconds0[cut, :].astype(F32) + seconds1[cut, :].astype(F32)
        ).astype(BF)

    loop(nd, blend)
    keep_mix = pltpu.make_async_copy(seconds1, mix_o, store_sem.at[1])
    keep_mix.start()
    scale = 1.0 + keep + keep * keep

    def rate(i, terms):
        cut = tile(i, step)
        projected = scale * tan0[:, cut] - fold(seconds1, cut)
        return terms + projected * (pulled[:, cut] * slopes[:, cut])

    terms = lax.fori_loop(0, hid // step, rate, jnp.zeros((rows, step), F32))
    for p in range(nf):
        one = jnp.sum(terms[p * acts : (p + 1) * acts], 0, keepdims=True)
        tally[p] = jnp.broadcast_to(jnp.sum(one, -1, keepdims=True), tally.shape[1:])
    votes = [
        remote(tally.at[f_peer(k)], tally_in.at[k], f_send.at[7, k], f_recv.at[7, k], (f_peer(k), d))
        for k in range(1, nf)
    ]
    value = tally[f]
    for k in range(1, nf):
        votes[k - 1].wait_recv()
        value = value + tally_in[k]
    score[...] = -value / (acts * math.sqrt(width * hid * nf))
    for copy in votes:
        copy.wait_send()
    keep_every.wait()
    keep_mix.wait()


def spread(
    nf, nd,
    noise_h, action_h, kv_h, flow, mask_h, w_up_h, w_down_h, grad_h,
    out, score,
    noise, action, kv, mask, w_up, w_down, grad, every, flipped, seconds, gram,
    slopes, curves, pulled, tan0, tan1, lhs, part, land0, land1, pair0, pair1,
    resid, tally, tally_in,
    load_sem, store_sem, f_send, f_recv, z_send, z_recv, x_send, x_recv, c_send, c_recv,
):
    acts, width = noise.shape
    hid = w_up.shape[1]
    rows = nf * acts
    total = nd * rows
    chips = nd // CORES
    pack = CORES * rows
    step = min(256, hid)
    wide = min(256, width)
    f = lax.axis_index("fsdp")
    d = lax.axis_index("dp")
    chip, core = d // CORES, d % CORES
    sibling = chip * CORES + (1 - core)

    def f_peer(k):
        return lax.rem(f + k, nf)

    def f_from(k):
        return lax.rem(f + nf - k, nf)

    def d_peer(k):
        return lax.rem(chip + k, chips) * CORES + core

    def chip_from(k):
        return lax.rem(chip + chips - k, chips)

    barrier = pltpu.get_barrier_semaphore()
    for k in range(1, nf):
        pl.semaphore_signal(barrier, inc=1, device_id=(f_peer(k), d), device_id_type=MESH)
    for k in range(1, chips):
        pl.semaphore_signal(barrier, inc=1, device_id=(f, d_peer(k)), device_id_type=MESH)
    pl.semaphore_signal(barrier, inc=1, device_id=(f, sibling), device_id_type=MESH)

    pairs = (
        (noise_h, noise), (action_h, action), (kv_h, kv), (mask_h, mask),
        (w_up_h, w_up), (grad_h, grad), (w_down_h, w_down),
    )
    loads = [pltpu.make_async_copy(src, dst, load_sem.at[i]) for i, (src, dst) in enumerate(pairs)]
    for load in loads:
        load.start()

    def remote(src, dst, send, recv, who):
        copy = pltpu.make_async_remote_copy(
            src_ref=src, dst_ref=dst, send_sem=send, recv_sem=recv, device_id=who, device_id_type=MESH
        )
        copy.start()
        return copy

    sent = []

    def scatter(phase, src, dst):
        return [
            remote(src(f_peer(k)), dst(k), f_send.at[phase, k], f_recv.at[phase, k], (f_peer(k), d))
            for k in range(1, nf)
        ]

    def block(g, kk, k):
        who = chip_from(kk) * CORES + core
        if g == 1:
            return pair0.at[who, :, tile(f_from(k), acts), :]
        at = pl.ds(pl.multiple_of(who * rows + f_from(k) * acts, acts), acts)
        return (every if g == 0 else pair1).at[at, :]

    across, to_core, along = {}, {}, {}

    def keep_copy(table, key, copy):
        table[key] = copy
        sent.append(copy)

    def share(g, kk):
        mine = block(g, kk, 0)
        for k in range(1, nf):
            keep_copy(across, (g, kk, k), remote(
                mine, mine, x_send.at[g, kk, k], x_recv.at[g, kk, k], (f_peer(k), d)
            ))
        pass_on(g, kk, 0)

    def pass_on(g, kk, k):
        mine = block(g, kk, k)
        keep_copy(to_core, (g, kk, k), remote(
            mine, mine, c_send.at[g, kk, k], c_recv.at[g, kk, k], (f, sibling)
        ))

    def begin(g):
        mine = block(g, 0, 0)
        for k in range(1, chips):
            keep_copy(along, (g, k), remote(
                mine, mine, z_send.at[g, k], z_recv.at[g, k], (f, d_peer(k))
            ))
        share(g, 0)

    def from_z(g):
        for kk in range(1, chips):
            along[g, kk].wait_recv()
            share(g, kk)

    def from_f(g, kk):
        for k in range(1, nf):
            across[g, kk, k].wait_recv()
            pass_on(g, kk, k)

    def from_core(g, kk):
        for k in range(nf):
            to_core[g, kk, k].wait_recv()

    for load in loads[:4]:
        load.wait()
    normed, left = attend(noise, action, kv, flow)
    resid[...] = left
    own = pl.ds(pl.multiple_of(d * rows + f * acts, acts), acts)
    every[own, :] = normed
    lane = lax.broadcasted_iota(jnp.int32, (acts, acts), 1)
    line = lax.broadcasted_iota(jnp.int32, (acts, acts), 0)
    valid = jnp.sum(
        jnp.where(lane == line, jnp.broadcast_to(mask[...].astype(F32), (acts, acts)), 0.0), -1, keepdims=True
    )
    pl.semaphore_wait(barrier, nf - 1 + chips)
    begin(0)
    group_at = tile(d, rows)

    def first(at, cut):
        group = every[at, :]
        pre = dot32(group, w_up[:, cut])
        tangent = dot32(group, grad[:, cut].astype(BF))
        sig = 1.0 / (1.0 + jnp.exp(-pre))
        slope = sig * (1.0 + pre * (1.0 - sig))
        slopes[at, cut] = slope
        curves[at, cut] = sig * (1.0 - sig) * (2.0 + pre * (1.0 - 2.0 * sig))
        tan0[at, cut] = tangent
        return pre * sig, slope * tangent

    def first_own(i):
        cut = tile(i, step)
        active, linear = first(group_at, cut)
        lhs[0:rows, cut] = active.astype(BF)
        lhs[rows : 2 * rows, cut] = linear.astype(BF)

    loads[4].wait()
    loads[5].wait()
    from_f(0, 0)
    loop(hid // step, first_own)
    from_z(0)
    loads[6].wait()

    def down(i):
        cut = tile(i, wide)
        part[:, cut] = dot32(lhs[...], w_down[:, cut]).astype(BF)

    loop(width // wide, down)

    def rows_of(p, q):
        return pl.ds(pl.multiple_of(q * rows + p * acts, acts), acts)

    outs = scatter(0, lambda p: part.at[rows_of(p, 0), :], lambda k: land0.at[k, 0:acts, :])
    moves = scatter(1, lambda p: part.at[rows_of(p, 1), :], lambda k: land0.at[k, acts : 2 * acts, :])

    def summed(copies, q, land, lo):
        value = part[rows_of(f, q), :].astype(F32)
        for k in range(1, nf):
            copies[k - 1].wait_recv()
            value = value + land[k, lo : lo + acts, :].astype(F32)
        return value

    def chunk(kk):
        return tile(chip_from(kk), pack)

    def rest(kk):
        from_core(0, kk)

        def body(i):
            first(chunk(kk), tile(i, step))

        loop(hid // step, body)

    rest(0)
    here = tile(f, acts)
    pair0[d, 0, here, :] = (valid * (resid[...] + summed(outs, 0, land0, 0))).astype(BF)
    pair0[d, 1, here, :] = (valid * summed(moves, 1, land0, acts)).astype(BF)
    begin(1)
    for kk in range(1, chips):
        from_f(0, kk)
    rest(1)
    from_z(1)
    for kk in range(2, chips):
        rest(kk)
    from_f(1, 0)

    def grams(i):
        cut = tile(i, pack)
        gram[cut, :] = (dot_t(every[cut, :], every[...]) / total).astype(BF)

    loop(chips, grams)

    def flip(i):
        cut = tile(i, wide)
        flipped[cut, :] = every[:, cut].T

    loop(width // wide, flip)

    def bend(kk):
        base = chip_from(kk) * CORES

        def body(i):
            cut = tile(i, step)
            tokens = pair0[pl.ds(base, CORES)].reshape(2 * pack, width)
            both = dot_t(tokens, w_down[cut, :])
            for c in range(CORES):
                at = tile(base + c, rows)
                pull = both[2 * c * rows : (2 * c + 1) * rows]
                push = both[(2 * c + 1) * rows : (2 * c + 2) * rows]
                pulled[at, cut] = pull
                seconds[0, at, cut] = (
                    push * slopes[at, cut] + pull * curves[at, cut] * tan0[at, cut]
                ).astype(BF)

        loop(hid // step, body)

    for kk in range(chips):
        if kk + 1 < chips:
            from_f(1, kk + 1)
        from_core(1, kk)
        bend(kk)

    def again(at, cut):
        tangent = (1.0 + keep) * tan0[at, cut] - dot32(gram[at, :], seconds[0, :, cut])
        tan1[at, cut] = tangent
        return tangent

    def again_own(i):
        cut = tile(i, step)
        lhs[0:rows, cut] = (slopes[group_at, cut] * again(group_at, cut)).astype(BF)

    loop(hid // step, again_own)
    for copy in outs + moves:
        copy.wait_send()

    def down_again(i):
        cut = tile(i, wide)
        part[0:rows, cut] = dot32(lhs[0:rows, :], w_down[:, cut]).astype(BF)

    loop(width // wide, down_again)
    moves1 = scatter(2, lambda p: part.at[rows_of(p, 0), :], lambda k: land1.at[k])
    sent.extend(moves1)

    def again_all(i):
        again(slice(None), tile(i, step))

    loop(hid // step, again_all)
    pair1[own, :] = (valid * summed(moves1, 0, land1, 0)).astype(BF)
    begin(2)

    def settle(i):
        cut = tile(i, wide)
        change = dot32(flipped[cut, :], seconds[0])
        grad[cut, :] = (1.0 + keep + keep * keep) * grad[cut, :] - (keep / total) * change

    half = max(1, width // wide // 2)
    pl.loop(0, half)(settle)
    from_z(2)
    pl.loop(half, width // wide)(settle)
    from_f(2, 0)

    def bend_again(kk):
        at = chunk(kk)

        def body(i):
            cut = tile(i, step)
            both = dot_t(pair1[at, :], w_down[cut, :])
            seconds[1, at, cut] = (
                both * slopes[at, cut] + pulled[at, cut] * curves[at, cut] * tan1[at, cut]
            ).astype(BF)

        loop(hid // step, body)

    for kk in range(chips):
        if kk + 1 < chips:
            from_f(2, kk + 1)
        from_core(2, kk)
        bend_again(kk)

    def rate(i, terms):
        cut = tile(i, step)
        projected = tan0[group_at, cut] + keep * tan1[group_at, cut]
        projected = projected - dot32(gram[group_at, :], seconds[1, :, cut])
        return terms + projected * (pulled[group_at, cut] * slopes[group_at, cut])

    terms = lax.fori_loop(0, hid // step, rate, jnp.zeros((rows, step), F32))
    for p in range(nf):
        one = jnp.sum(terms[p * acts : (p + 1) * acts], 0, keepdims=True)
        tally[p] = jnp.broadcast_to(jnp.sum(one, -1, keepdims=True), tally.shape[1:])
    votes = scatter(3, lambda p: tally.at[p], lambda k: tally_in.at[k])
    sent.extend(votes)
    stores = []
    for i in range(width // wide):
        cut = pl.ds(i * wide, wide)
        grad[cut, :] = grad[cut, :] - dot32(flipped[cut, :], seconds[1]) / total
        stores.append(pltpu.make_async_copy(grad.at[cut, :], out.at[cut, :], store_sem.at[i]))
        stores[-1].start()
    value = tally[f]
    for k in range(1, nf):
        votes[k - 1].wait_recv()
        value = value + tally_in[k]
    score[...] = -value / (acts * math.sqrt(width * hid * nf))
    for copy in sent:
        copy.wait_send()
    for store in stores:
        store.wait()


def spread_call(nf, nd, noise, action, kv, flow, mask, w_up, w_down, grad):
    acts, width = noise.shape
    hid = w_up.shape[1]
    rows = nf * acts
    total = nd * rows
    chips = nd // CORES
    vmem = pl.BlockSpec(memory_space=pltpu.VMEM)
    anywhere = pl.BlockSpec(memory_space=pl.ANY)
    dma = pltpu.SemaphoreType.DMA
    far = pl.BlockSpec(memory_space=pltpu.HBM)
    half, full = (lambda *s: pltpu.VMEM(s, BF)), (lambda *s: pltpu.VMEM(s, F32))
    vector, score = pl.pallas_call(
        functools.partial(spread, nf, nd),
        out_shape=(jax.ShapeDtypeStruct((width, hid), F32), jax.ShapeDtypeStruct((8, 128), F32)),
        in_specs=[far] * 3 + [pl.BlockSpec(memory_space=pltpu.SMEM)] + [far] * 4,
        out_specs=(anywhere, vmem),
        scratch_shapes=[
            half(acts, width), half(acts, width), half(*kv.shape), pltpu.VMEM((1, acts), jnp.int32),
            half(width, hid), half(hid, width), full(width, hid),
            half(total, width), half(width, total), half(2, total, hid), half(total, total),
        ] + [full(total, hid)] * 5 + [
            half(2 * rows, hid), half(2 * rows, width), half(nf, 2 * acts, width), half(nf, acts, width),
            half(nd, 2, rows, width), half(total, width),
            full(acts, width), full(nf, 8, 128), full(nf, 8, 128),
            dma((7,)), dma((max(1, width // 256),)), dma((4, nf)), dma((4, nf)),
            dma((3, chips)), dma((3, chips)), dma((3, chips, nf)), dma((3, chips, nf)),
            dma((3, chips, nf)), dma((3, chips, nf)),
        ],
        compiler_params=pltpu.CompilerParams(
            collective_id=0, has_side_effects=True, vmem_limit_bytes=60 * 1024 * 1024
        ),
        name="lissa",
    )(noise, action, kv, flow, mask.reshape(1, acts), w_up, w_down, grad)
    return vector, score[0, 0:1]


def finish(total, every, mix, grad, out):
    change = lax.dot_general(
        every[...], mix[...], (((0,), (0,)), ((), ())), preferred_element_type=F32
    )
    out[...] = (1.0 + keep + keep * keep) * grad[...] - change / total


def shards(nf, nd, noise, action, kv, flow, mask, w_up, w_down, grad):
    acts, width = noise.shape
    hid = w_up.shape[1]
    rows = nf * acts
    total = nd * rows
    if total <= 512:
        return spread_call(nf, nd, noise, action, kv, flow, mask, w_up, w_down, grad)
    vmem = pl.BlockSpec(memory_space=pltpu.VMEM)
    anywhere = pl.BlockSpec(memory_space=pl.ANY)
    dma = pltpu.SemaphoreType.DMA
    chips = nd // CORES
    every, mix, score = pl.pallas_call(
        functools.partial(kernel, nf, nd),
        out_shape=(
            jax.ShapeDtypeStruct((total, width), BF),
            jax.ShapeDtypeStruct((total, hid), BF),
            jax.ShapeDtypeStruct((8, 128), F32),
        ),
        in_specs=[
            vmem, vmem, vmem, pl.BlockSpec(memory_space=pltpu.SMEM), vmem, anywhere, anywhere, anywhere,
        ],
        out_specs=(anywhere, anywhere, vmem),
        scratch_shapes=[
            pltpu.VMEM((width, hid), BF),
            pltpu.VMEM((hid, width), BF),
            pltpu.VMEM((width, hid), F32),
            pltpu.VMEM((total, width), BF),
            pltpu.VMEM((total, hid), BF),
            pltpu.VMEM((total, hid), BF),
            pltpu.VMEM((rows, total), BF),
            pltpu.VMEM((rows, hid), F32),
            pltpu.VMEM((rows, hid), F32),
            pltpu.VMEM((rows, hid), F32),
            pltpu.VMEM((rows, hid), F32),
            pltpu.VMEM((rows, hid), F32),
            pltpu.VMEM((2 * rows, hid), BF),
            pltpu.VMEM((2 * rows, width), BF),
            pltpu.VMEM((nf, 2 * acts, width), BF),
            pltpu.VMEM((nf, acts, width), BF),
            pltpu.VMEM((2 * rows, width), BF),
            pltpu.VMEM((rows, width), BF),
            pltpu.VMEM((acts, width), F32),
            pltpu.VMEM((nf, 8, 128), F32),
            pltpu.VMEM((nf, 8, 128), F32),
            dma((3,)),
            dma((2,)),
            dma((8, nf)),
            dma((8, nf)),
            dma((3, chips)),
            dma((3, chips)),
            dma((3, chips)),
            dma((3, chips)),
        ],
        compiler_params=pltpu.CompilerParams(
            collective_id=0, has_side_effects=True, vmem_limit_bytes=52 * 1024 * 1024
        ),
        name="lissa",
    )(noise, action, kv, flow, mask.reshape(1, acts), w_up, w_down, grad)
    strip = 128
    vector = pl.pallas_call(
        functools.partial(finish, total),
        out_shape=jax.ShapeDtypeStruct((width, hid), F32),
        grid=(width // strip,),
        in_specs=[
            pl.BlockSpec((total, strip), lambda i: (0, i)),
            pl.BlockSpec((total, hid), lambda i: (0, 0)),
            pl.BlockSpec((strip, hid), lambda i: (i, 0)),
        ],
        out_specs=pl.BlockSpec((strip, hid), lambda i: (i, 0)),
        compiler_params=pltpu.CompilerParams(vmem_limit_bytes=40 * 1024 * 1024),
        name="finish",
    )(every, mix, grad)
    return vector, score[0, 0:1]


def solution(mesh):
    placed = (
        P(("fsdp", "dp"), None),
        P(("fsdp", "dp"), None),
        P(None, ("fsdp", "dp"), None, None),
        P(("fsdp", "dp")),
        P(("fsdp", "dp")),
        P(None, "fsdp"),
        P("fsdp", None),
        P(None, "fsdp"),
    )
    return jax.shard_map(
        functools.partial(shards, mesh.shape["fsdp"], mesh.shape["dp"]),
        mesh=mesh,
        in_specs=placed,
        out_specs=(P(None, "fsdp"), P(("fsdp", "dp"))),
        check_vma=False,
    )
```

```python
import functools
import math

import jax
import jax.numpy as jnp
from jax import lax
from jax.experimental import pallas as pl
from jax.experimental.pallas import tpu as pltpu
from jax.sharding import PartitionSpec as P

STEPS_T = 10
CORES = 2

epsilon = 1e-06
sharpness_divisor = 6.0
keep = 1.0 - 0.01

BF = jnp.bfloat16
F32 = jnp.float32
MESH = pl.DeviceIdType.MESH


def dot32(a, b):
    return jnp.dot(a, b, preferred_element_type=F32)


def dot_t(a, b):
    return lax.dot_general(a, b, (((1,), (1,)), ((), ())), preferred_element_type=F32)


def loop(count, body):
    if count == 1:
        body(0)
    else:
        pl.loop(0, count)(body)


def tile(i, size):
    return pl.ds(pl.multiple_of(i * size, size), size)


def attend(noise, action, kv, flow):
    acts, width = noise.shape
    span = kv.shape[3]
    heads = width // span
    time = (flow[0].astype(F32) + 1.0) / (STEPS_T + 1.0)
    noisy = noise[...].astype(F32)
    clean = action[...].astype(F32)
    inputs = time * noisy + (1.0 - time) * clean
    queries = jnp.concatenate([inputs[:, h * span : (h + 1) * span] for h in range(heads)], 0)
    queries = queries * lax.rsqrt(jnp.mean(queries * queries, -1, keepdims=True) + epsilon)
    keys = kv[0, 0].astype(F32)
    keys = keys * lax.rsqrt(jnp.mean(keys * keys, -1, keepdims=True) + epsilon)
    expo = jnp.exp(dot_t(queries.astype(BF), keys.astype(BF)) * (sharpness_divisor / span))
    weights = (expo / jnp.sum(expo, -1, keepdims=True)).astype(BF)
    mixed = dot32(weights, kv[1, 0])
    mixed = jnp.concatenate([mixed[h * acts : (h + 1) * acts] for h in range(heads)], 1)
    hidden = inputs + mixed
    normed = hidden * lax.rsqrt(jnp.mean(hidden * hidden, -1, keepdims=True) + epsilon)
    return normed.astype(BF), hidden - (noisy - clean)


def kernel(
    nf, nd,
    noise, action, kv, flow, mask, w_up_h, w_down_h, grad_h,
    every_o, mix_o, score,
    w_up, w_down, grad, every, seconds0, seconds1, gram,
    slopes, curves, pulled, tan0, tan1, lhs, part, land0, land1, pair0, pair1,
    resid, tally, tally_in,
    load_sem, store_sem, f_send, f_recv, z_send, z_recv, c_send, c_recv,
):
    acts, width = noise.shape
    hid = w_up.shape[1]
    rows = nf * acts
    total = nd * rows
    chips = nd // CORES
    f = lax.axis_index("fsdp")
    d = lax.axis_index("dp")
    chip, core = d // CORES, d % CORES
    sibling = chip * CORES + (1 - core)

    def f_peer(k):
        return lax.rem(f + k, nf)

    def d_peer(k):
        return lax.rem(chip + k, chips) * CORES + core

    def d_from(k):
        return lax.rem(chip + chips - k, chips) * CORES + core

    barrier = pltpu.get_barrier_semaphore()
    for k in range(1, nf):
        pl.semaphore_signal(barrier, inc=1, device_id=(f_peer(k), d), device_id_type=MESH)
    for k in range(1, chips):
        pl.semaphore_signal(barrier, inc=1, device_id=(f, d_peer(k)), device_id_type=MESH)
    pl.semaphore_signal(barrier, inc=1, device_id=(f, sibling), device_id_type=MESH)

    loads = [
        pltpu.make_async_copy(src, dst, load_sem.at[i])
        for i, (src, dst) in enumerate(((w_up_h, w_up), (grad_h, grad), (w_down_h, w_down)))
    ]
    for load in loads:
        load.start()

    def remote(src, dst, send, recv, who):
        copy = pltpu.make_async_remote_copy(
            src_ref=src, dst_ref=dst, send_sem=send, recv_sem=recv, device_id=who, device_id_type=MESH
        )
        copy.start()
        return copy

    sent = []

    def fsdp(phase, src, dst):
        copies = [
            remote(src(f_peer(k)), dst(k), f_send.at[phase, k], f_recv.at[phase, k], (f_peer(k), d))
            for k in range(1, nf)
        ]
        if phase not in (1, 2):
            sent.extend(copies)
        return copies

    def landed(copies):
        for copy in copies:
            copy.wait_recv()

    def dp_start(phase, buf):
        mine = buf.at[tile(d, rows), :]
        z = [
            remote(mine, mine, z_send.at[phase, k], z_recv.at[phase, k], (f, d_peer(k)))
            for k in range(1, chips)
        ]
        c = [remote(mine, mine, c_send.at[phase, 0], c_recv.at[phase, 0], (f, sibling))]
        sent.extend(z)
        sent.extend(c)
        return z, c

    def dp_forward(phase, buf, z, c):
        for k in range(1, chips):
            z[k - 1].wait_recv()
            block = buf.at[tile(d_from(k), rows), :]
            copy = remote(block, block, c_send.at[phase, k], c_recv.at[phase, k], (f, sibling))
            sent.append(copy)
            c.append(copy)

    normed, left = attend(noise, action, kv, flow)
    resid[...] = left
    own = pl.ds(pl.multiple_of(d * rows + f * acts, acts), acts)
    every[own, :] = normed
    lane = lax.broadcasted_iota(jnp.int32, (acts, acts), 1)
    line = lax.broadcasted_iota(jnp.int32, (acts, acts), 0)
    valid = jnp.sum(
        jnp.where(lane == line, jnp.broadcast_to(mask[...].astype(F32), (acts, acts)), 0.0), -1, keepdims=True
    )
    pl.semaphore_wait(barrier, nf - 1 + chips)

    mine = every.at[own, :]
    landed(fsdp(0, lambda p: mine, lambda k: mine))
    group_at = tile(d, rows)
    z_n, c_n = dp_start(0, every)

    loads[0].wait()
    loads[1].wait()
    step = min(256, hid)

    def first(i):
        cut = tile(i, step)
        group = every[group_at, :]
        pre = dot32(group, w_up[:, cut])
        tangent = dot32(group, grad[:, cut].astype(BF))
        sig = 1.0 / (1.0 + jnp.exp(-pre))
        slope = sig * (1.0 + pre * (1.0 - sig))
        slopes[:, cut] = slope
        curves[:, cut] = sig * (1.0 - sig) * (2.0 + pre * (1.0 - 2.0 * sig))
        tan0[:, cut] = tangent
        lhs[0:rows, cut] = (pre * sig).astype(BF)
        lhs[rows : 2 * rows, cut] = (slope * tangent).astype(BF)

    loop(hid // step, first)
    loads[2].wait()
    wide = min(256, width)

    def down(i):
        cut = tile(i, wide)
        part[:, cut] = dot32(lhs[...], w_down[:, cut]).astype(BF)

    loop(width // wide, down)

    def rows_of(p, q):
        return pl.ds(pl.multiple_of(q * rows + p * acts, acts), acts)

    outs = fsdp(1, lambda p: part.at[rows_of(p, 0), :], lambda k: land0.at[k, 0:acts, :])
    moves = fsdp(2, lambda p: part.at[rows_of(p, 1), :], lambda k: land0.at[k, acts : 2 * acts, :])

    def summed(copies, q, land, lo):
        value = part[rows_of(f, q), :].astype(F32)
        for k in range(1, nf):
            copies[k - 1].wait_recv()
            value = value + land[k, lo : lo + acts, :].astype(F32)
        return value

    err = (valid * (resid[...] + summed(outs, 0, land0, 0))).astype(BF)
    pair0[rows_of(f, 0), :] = err
    errs = fsdp(3, lambda p: pair0.at[rows_of(f, 0), :], lambda k: pair0.at[rows_of(f, 0), :])
    pair0[rows_of(f, 1), :] = (valid * summed(moves, 1, land0, acts)).astype(BF)
    merrs = fsdp(4, lambda p: pair0.at[rows_of(f, 1), :], lambda k: pair0.at[rows_of(f, 1), :])
    dp_forward(0, every, z_n, c_n)
    landed(errs)
    landed(merrs)

    def bend(i):
        cut = tile(i, step)
        both = dot_t(pair0[...], w_down[cut, :])
        pull = both[0:rows]
        pulled[:, cut] = pull
        seconds0[group_at, cut] = (
            both[rows : 2 * rows] * slopes[:, cut] + pull * curves[:, cut] * tan0[:, cut]
        ).astype(BF)

    loop(hid // step, bend)
    z_0, c_0 = dp_start(1, seconds0)
    landed(c_n)
    keep_every = pltpu.make_async_copy(every, every_o, store_sem.at[0])
    keep_every.start()
    chunk = min(512, total)

    def grams(i):
        cut = tile(i, chunk)
        gram[:, cut] = (dot_t(every[group_at, :], every[cut, :]) / total).astype(BF)

    loop(total // chunk, grams)
    dp_forward(1, seconds0, z_0, c_0)
    landed(c_0)

    def fold(seconds, cut):
        if total == chunk:
            return dot32(gram[...], seconds[:, cut])
        return lax.fori_loop(
            0,
            total // chunk,
            lambda j, v: v + dot32(gram[:, tile(j, chunk)], seconds[tile(j, chunk), cut]),
            jnp.zeros((rows, step), F32),
        )

    def again(i):
        cut = tile(i, step)
        tangent = (1.0 + keep) * tan0[:, cut] - fold(seconds0, cut)
        tan1[:, cut] = tangent
        lhs[0:rows, cut] = (slopes[:, cut] * tangent).astype(BF)

    loop(hid // step, again)
    for copy in outs + moves:
        copy.wait_send()

    def down_again(i):
        cut = tile(i, wide)
        part[0:rows, cut] = dot32(lhs[0:rows, :], w_down[:, cut]).astype(BF)

    loop(width // wide, down_again)
    moves1 = fsdp(5, lambda p: part.at[rows_of(p, 0), :], lambda k: land1.at[k])
    pair1[rows_of(f, 0), :] = (valid * summed(moves1, 0, land1, 0)).astype(BF)
    landed(fsdp(6, lambda p: pair1.at[rows_of(f, 0), :], lambda k: pair1.at[rows_of(f, 0), :]))

    def bend_again(i):
        cut = tile(i, step)
        both = dot_t(pair1[...], w_down[cut, :])
        seconds1[group_at, cut] = (
            both * slopes[:, cut] + pulled[:, cut] * curves[:, cut] * tan1[:, cut]
        ).astype(BF)

    loop(hid // step, bend_again)
    z_1, c_1 = dp_start(2, seconds1)
    dp_forward(2, seconds1, z_1, c_1)
    landed(c_1)
    for copy in sent:
        copy.wait_send()

    def blend(i):
        cut = tile(i, rows)
        seconds1[cut, :] = (
            keep * seconds0[cut, :].astype(F32) + seconds1[cut, :].astype(F32)
        ).astype(BF)

    loop(nd, blend)
    keep_mix = pltpu.make_async_copy(seconds1, mix_o, store_sem.at[1])
    keep_mix.start()
    scale = 1.0 + keep + keep * keep

    def rate(i, terms):
        cut = tile(i, step)
        projected = scale * tan0[:, cut] - fold(seconds1, cut)
        return terms + projected * (pulled[:, cut] * slopes[:, cut])

    terms = lax.fori_loop(0, hid // step, rate, jnp.zeros((rows, step), F32))
    for p in range(nf):
        one = jnp.sum(terms[p * acts : (p + 1) * acts], 0, keepdims=True)
        tally[p] = jnp.broadcast_to(jnp.sum(one, -1, keepdims=True), tally.shape[1:])
    votes = [
        remote(tally.at[f_peer(k)], tally_in.at[k], f_send.at[7, k], f_recv.at[7, k], (f_peer(k), d))
        for k in range(1, nf)
    ]
    value = tally[f]
    for k in range(1, nf):
        votes[k - 1].wait_recv()
        value = value + tally_in[k]
    score[...] = -value / (acts * math.sqrt(width * hid * nf))
    for copy in votes:
        copy.wait_send()
    keep_every.wait()
    keep_mix.wait()


def spread(
    nf, nd,
    noise_h, action_h, kv_h, flow, mask_h, w_up_h, w_down_h, grad_h,
    out, score,
    noise, action, kv, mask, w_up, w_down, grad, gradb, every, flipped, seconds, gram,
    slopes, curves, pulled, tan0, tan1, lhs, part, land0, land1, pair0, pair1,
    resid, tally, tally_in,
    load_sem, store_sem, f_send, f_recv, z_send, z_recv, x_send, x_recv, c_send, c_recv,
):
    acts, width = noise.shape
    hid = w_up.shape[1]
    rows = nf * acts
    total = nd * rows
    chips = nd // CORES
    pack = CORES * rows
    step = min(256, hid)
    wide = min(256, width)
    f = lax.axis_index("fsdp")
    d = lax.axis_index("dp")
    chip, core = d // CORES, d % CORES
    sibling = chip * CORES + (1 - core)

    def f_peer(k):
        return lax.rem(f + k, nf)

    def f_from(k):
        return lax.rem(f + nf - k, nf)

    def d_peer(k):
        return lax.rem(chip + k, chips) * CORES + core

    def chip_from(k):
        return lax.rem(chip + chips - k, chips)

    barrier = pltpu.get_barrier_semaphore()
    for k in range(1, nf):
        pl.semaphore_signal(barrier, inc=1, device_id=(f_peer(k), d), device_id_type=MESH)
    for k in range(1, chips):
        pl.semaphore_signal(barrier, inc=1, device_id=(f, d_peer(k)), device_id_type=MESH)
    pl.semaphore_signal(barrier, inc=1, device_id=(f, sibling), device_id_type=MESH)

    pairs = (
        (noise_h, noise), (action_h, action), (kv_h, kv), (mask_h, mask),
        (w_up_h, w_up), (grad_h, grad), (w_down_h, w_down),
    )
    loads = [pltpu.make_async_copy(src, dst, load_sem.at[i]) for i, (src, dst) in enumerate(pairs)]
    for load in loads:
        load.start()

    def remote(src, dst, send, recv, who):
        copy = pltpu.make_async_remote_copy(
            src_ref=src, dst_ref=dst, send_sem=send, recv_sem=recv, device_id=who, device_id_type=MESH
        )
        copy.start()
        return copy

    sent = []

    def scatter(phase, src, dst):
        return [
            remote(src(f_peer(k)), dst(k), f_send.at[phase, k], f_recv.at[phase, k], (f_peer(k), d))
            for k in range(1, nf)
        ]

    def block(g, kk, k):
        who = chip_from(kk) * CORES + core
        if g == 1:
            return pair0.at[who, :, tile(f_from(k), acts), :]
        at = pl.ds(pl.multiple_of(who * rows + f_from(k) * acts, acts), acts)
        return (every if g == 0 else pair1).at[at, :]

    across, to_core, along = {}, {}, {}

    def keep_copy(table, key, copy):
        table[key] = copy
        sent.append(copy)

    def share(g, kk):
        mine = block(g, kk, 0)
        for k in range(1, nf):
            keep_copy(across, (g, kk, k), remote(
                mine, mine, x_send.at[g, kk, k], x_recv.at[g, kk, k], (f_peer(k), d)
            ))

    def begin(g):
        mine = block(g, 0, 0)
        for k in range(1, chips):
            keep_copy(along, (g, k), remote(
                mine, mine, z_send.at[g, k], z_recv.at[g, k], (f, d_peer(k))
            ))
        share(g, 0)

    def from_z(g):
        for kk in range(1, chips):
            along[g, kk].wait_recv()
            share(g, kk)

    def from_f(g, kk):
        for k in range(1, nf):
            across[g, kk, k].wait_recv()
        who = chip_from(kk) * CORES + core
        mine = pair0.at[who] if g == 1 else (every if g == 0 else pair1).at[tile(who, rows), :]
        keep_copy(to_core, (g, kk), remote(
            mine, mine, c_send.at[g, kk], c_recv.at[g, kk], (f, sibling)
        ))

    def from_core(g, kk):
        to_core[g, kk].wait_recv()

    for load in loads[:4]:
        load.wait()
    normed, left = attend(noise, action, kv, flow)
    resid[...] = left
    own = pl.ds(pl.multiple_of(d * rows + f * acts, acts), acts)
    every[own, :] = normed
    lane = lax.broadcasted_iota(jnp.int32, (acts, acts), 1)
    line = lax.broadcasted_iota(jnp.int32, (acts, acts), 0)
    valid = jnp.sum(
        jnp.where(lane == line, jnp.broadcast_to(mask[...].astype(F32), (acts, acts)), 0.0), -1, keepdims=True
    )
    pl.semaphore_wait(barrier, nf - 1 + chips)
    begin(0)
    group_at = tile(d, rows)

    def first(at, cut):
        group = every[at, :]
        pre = dot32(group, w_up[:, cut])
        tangent = dot32(group, gradb[:, cut])
        sig = 1.0 / (1.0 + jnp.exp(-pre))
        slope = sig * (1.0 + pre * (1.0 - sig))
        slopes[at, cut] = slope
        curves[at, cut] = sig * (1.0 - sig) * (2.0 + pre * (1.0 - 2.0 * sig))
        tan0[at, cut] = tangent
        return pre * sig, slope * tangent

    def first_own(i):
        cut = tile(i, step)
        active, linear = first(group_at, cut)
        lhs[0:rows, cut] = active.astype(BF)
        lhs[rows : 2 * rows, cut] = linear.astype(BF)

    loads[5].wait()

    def narrow(i):
        cut = tile(i, wide)
        gradb[cut, :] = grad[cut, :].astype(BF)

    loop(width // wide, narrow)
    loads[4].wait()
    from_f(0, 0)
    first_own(0)
    from_z(0)
    if hid > step:
        pl.loop(1, hid // step)(first_own)
    loads[6].wait()

    def down(i):
        cut = tile(i, wide)
        part[:, cut] = dot32(lhs[...], w_down[:, cut]).astype(BF)

    loop(width // wide, down)

    def rows_of(p, q):
        return pl.ds(pl.multiple_of(q * rows + p * acts, acts), acts)

    outs = scatter(0, lambda p: part.at[rows_of(p, 0), :], lambda k: land0.at[k, 0:acts, :])
    moves = scatter(1, lambda p: part.at[rows_of(p, 1), :], lambda k: land0.at[k, acts : 2 * acts, :])

    def summed(copies, q, land, lo):
        value = part[rows_of(f, q), :].astype(F32)
        for k in range(1, nf):
            copies[k - 1].wait_recv()
            value = value + land[k, lo : lo + acts, :].astype(F32)
        return value

    def chunk(kk):
        return tile(chip_from(kk), pack)

    def rest(kk):
        from_core(0, kk)

        def body(i):
            first(chunk(kk), tile(i, step))

        loop(hid // step, body)

    rest(0)
    here = tile(f, acts)
    pair0[d, 0, here, :] = (valid * (resid[...] + summed(outs, 0, land0, 0))).astype(BF)
    pair0[d, 1, here, :] = (valid * summed(moves, 1, land0, acts)).astype(BF)
    begin(1)
    for kk in range(1, chips):
        from_f(0, kk)
    rest(1)
    from_z(1)
    for kk in range(2, chips):
        rest(kk)
    from_f(1, 0)

    def grams(i):
        cut = tile(i, pack)
        gram[cut, :] = (dot_t(every[cut, :], every[...]) / total).astype(BF)

    loop(chips, grams)

    def flip(i):
        cut = tile(i, wide)
        flipped[cut, :] = every[:, cut].T

    loop(width // wide, flip)

    def bend(kk):
        base = chip_from(kk) * CORES

        def body(i):
            cut = tile(i, step)
            tokens = pair0[pl.ds(base, CORES)].reshape(2 * pack, width)
            both = dot_t(tokens, w_down[cut, :])
            for c in range(CORES):
                at = tile(base + c, rows)
                pull = both[2 * c * rows : (2 * c + 1) * rows]
                push = both[(2 * c + 1) * rows : (2 * c + 2) * rows]
                pulled[at, cut] = pull
                seconds[0, at, cut] = (
                    push * slopes[at, cut] + pull * curves[at, cut] * tan0[at, cut]
                ).astype(BF)

        loop(hid // step, body)

    for kk in range(chips):
        if kk + 1 < chips:
            from_f(1, kk + 1)
        from_core(1, kk)
        bend(kk)

    def again(at, cut):
        tangent = (1.0 + keep) * tan0[at, cut] - dot32(gram[at, :], seconds[0, :, cut])
        tan1[at, cut] = tangent
        return tangent

    def again_own(i):
        cut = tile(i, step)
        lhs[0:rows, cut] = (slopes[group_at, cut] * again(group_at, cut)).astype(BF)

    loop(hid // step, again_own)
    for copy in outs + moves:
        copy.wait_send()

    def down_again(i):
        cut = tile(i, wide)
        part[0:rows, cut] = dot32(lhs[0:rows, :], w_down[:, cut]).astype(BF)

    loop(width // wide, down_again)
    moves1 = scatter(2, lambda p: part.at[rows_of(p, 0), :], lambda k: land1.at[k])
    sent.extend(moves1)

    def again_all(i):
        again(slice(None), tile(i, step))

    loop(hid // step, again_all)
    pair1[own, :] = (valid * summed(moves1, 0, land1, 0)).astype(BF)
    begin(2)

    def settle(i):
        cut = tile(i, wide)
        change = dot32(flipped[cut, :], seconds[0])
        grad[cut, :] = (1.0 + keep + keep * keep) * grad[cut, :] - (keep / total) * change

    half = max(1, width // wide // 2)
    pl.loop(0, half)(settle)
    from_z(2)
    pl.loop(half, width // wide)(settle)
    from_f(2, 0)

    def bend_again(kk):
        at = chunk(kk)

        def body(i):
            cut = tile(i, step)
            both = dot_t(pair1[at, :], w_down[cut, :])
            seconds[1, at, cut] = (
                both * slopes[at, cut] + pulled[at, cut] * curves[at, cut] * tan1[at, cut]
            ).astype(BF)

        loop(hid // step, body)

    for kk in range(chips):
        if kk + 1 < chips:
            from_f(2, kk + 1)
        from_core(2, kk)
        bend_again(kk)

    def rate(i, terms):
        cut = tile(i, step)
        projected = tan0[group_at, cut] + keep * tan1[group_at, cut]
        projected = projected - dot32(gram[group_at, :], seconds[1, :, cut])
        return terms + projected * (pulled[group_at, cut] * slopes[group_at, cut])

    terms = lax.fori_loop(0, hid // step, rate, jnp.zeros((rows, step), F32))
    for p in range(nf):
        one = jnp.sum(terms[p * acts : (p + 1) * acts], 0, keepdims=True)
        tally[p] = jnp.broadcast_to(jnp.sum(one, -1, keepdims=True), tally.shape[1:])
    votes = scatter(3, lambda p: tally.at[p], lambda k: tally_in.at[k])
    sent.extend(votes)
    stores = []
    for i in range(width // wide):
        cut = pl.ds(i * wide, wide)
        grad[cut, :] = grad[cut, :] - dot32(flipped[cut, :], seconds[1]) * (1.0 / total)
        stores.append(pltpu.make_async_copy(grad.at[cut, :], out.at[cut, :], store_sem.at[i]))
        stores[-1].start()
    value = tally[f]
    for k in range(1, nf):
        votes[k - 1].wait_recv()
        value = value + tally_in[k]
    score[...] = -value / (acts * math.sqrt(width * hid * nf))
    for copy in sent:
        copy.wait_send()
    for store in stores:
        store.wait()


def hand_out(held, tally, out, score, sem):
    parts = sem.shape[0]
    high = out.shape[0] // parts
    copies = [
        pltpu.make_async_copy(
            held.at[pl.ds(i * high, high), :], out.at[pl.ds(i * high, high), :], sem.at[i]
        )
        for i in range(parts)
    ]
    for copy in copies:
        copy.start()
    score[0] = tally[0, 0]
    for copy in copies:
        copy.wait()


def spread_call(nf, nd, noise, action, kv, flow, mask, w_up, w_down, grad):
    acts, width = noise.shape
    hid = w_up.shape[1]
    rows = nf * acts
    total = nd * rows
    chips = nd // CORES
    vmem = pl.BlockSpec(memory_space=pltpu.VMEM)
    anywhere = pl.BlockSpec(memory_space=pl.ANY)
    dma = pltpu.SemaphoreType.DMA
    half, full = (lambda *s: pltpu.VMEM(s, BF)), (lambda *s: pltpu.VMEM(s, F32))
    vector, score = pl.pallas_call(
        functools.partial(spread, nf, nd),
        out_shape=(jax.ShapeDtypeStruct((width, hid), F32), jax.ShapeDtypeStruct((8, 128), F32)),
        in_specs=[anywhere] * 3 + [pl.BlockSpec(memory_space=pltpu.SMEM)] + [anywhere] * 4,
        out_specs=(anywhere, vmem),
        scratch_shapes=[
            half(acts, width), half(acts, width), half(*kv.shape), pltpu.VMEM((1, acts), jnp.int32),
            half(width, hid), half(hid, width), full(width, hid), half(width, hid),
            half(total, width), half(width, total), half(2, total, hid), half(total, total),
        ] + [full(total, hid)] * 5 + [
            half(2 * rows, hid), half(2 * rows, width), half(nf, 2 * acts, width), half(nf, acts, width),
            half(nd, 2, rows, width), half(total, width),
            full(acts, width), full(nf, 8, 128), full(nf, 8, 128),
            dma((7,)), dma((max(1, width // 256),)), dma((4, nf)), dma((4, nf)),
            dma((3, chips)), dma((3, chips)), dma((3, chips, nf)), dma((3, chips, nf)),
            dma((3, chips)), dma((3, chips)),
        ],
        compiler_params=pltpu.CompilerParams(
            collective_id=0, has_side_effects=True, vmem_limit_bytes=60 * 1024 * 1024
        ),
        name="lissa",
    )(noise, action, kv, flow, mask.reshape(1, acts), w_up, w_down, grad)
    return pl.pallas_call(
        hand_out,
        out_shape=(jax.ShapeDtypeStruct((width, hid), F32), jax.ShapeDtypeStruct((1,), F32)),
        in_specs=[anywhere, vmem],
        out_specs=(anywhere, pl.BlockSpec(memory_space=pltpu.SMEM)),
        scratch_shapes=[dma((4,))],
        compiler_params=pltpu.CompilerParams(vmem_limit_bytes=60 * 1024 * 1024),
        name="hand_out",
    )(vector, score)


def finish(total, every, mix, grad, out):
    change = lax.dot_general(
        every[...], mix[...], (((0,), (0,)), ((), ())), preferred_element_type=F32
    )
    out[...] = (1.0 + keep + keep * keep) * grad[...] - change / total


def shards(nf, nd, noise, action, kv, flow, mask, w_up, w_down, grad):
    acts, width = noise.shape
    hid = w_up.shape[1]
    rows = nf * acts
    total = nd * rows
    if total <= 512:
        return spread_call(nf, nd, noise, action, kv, flow, mask, w_up, w_down, grad)
    vmem = pl.BlockSpec(memory_space=pltpu.VMEM)
    anywhere = pl.BlockSpec(memory_space=pl.ANY)
    dma = pltpu.SemaphoreType.DMA
    chips = nd // CORES
    every, mix, score = pl.pallas_call(
        functools.partial(kernel, nf, nd),
        out_shape=(
            jax.ShapeDtypeStruct((total, width), BF),
            jax.ShapeDtypeStruct((total, hid), BF),
            jax.ShapeDtypeStruct((8, 128), F32),
        ),
        in_specs=[
            vmem, vmem, vmem, pl.BlockSpec(memory_space=pltpu.SMEM), vmem, anywhere, anywhere, anywhere,
        ],
        out_specs=(anywhere, anywhere, vmem),
        scratch_shapes=[
            pltpu.VMEM((width, hid), BF),
            pltpu.VMEM((hid, width), BF),
            pltpu.VMEM((width, hid), F32),
            pltpu.VMEM((total, width), BF),
            pltpu.VMEM((total, hid), BF),
            pltpu.VMEM((total, hid), BF),
            pltpu.VMEM((rows, total), BF),
            pltpu.VMEM((rows, hid), F32),
            pltpu.VMEM((rows, hid), F32),
            pltpu.VMEM((rows, hid), F32),
            pltpu.VMEM((rows, hid), F32),
            pltpu.VMEM((rows, hid), F32),
            pltpu.VMEM((2 * rows, hid), BF),
            pltpu.VMEM((2 * rows, width), BF),
            pltpu.VMEM((nf, 2 * acts, width), BF),
            pltpu.VMEM((nf, acts, width), BF),
            pltpu.VMEM((2 * rows, width), BF),
            pltpu.VMEM((rows, width), BF),
            pltpu.VMEM((acts, width), F32),
            pltpu.VMEM((nf, 8, 128), F32),
            pltpu.VMEM((nf, 8, 128), F32),
            dma((3,)),
            dma((2,)),
            dma((8, nf)),
            dma((8, nf)),
            dma((3, chips)),
            dma((3, chips)),
            dma((3, chips)),
            dma((3, chips)),
        ],
        compiler_params=pltpu.CompilerParams(
            collective_id=0, has_side_effects=True, vmem_limit_bytes=52 * 1024 * 1024
        ),
        name="lissa",
    )(noise, action, kv, flow, mask.reshape(1, acts), w_up, w_down, grad)
    strip = 128
    vector = pl.pallas_call(
        functools.partial(finish, total),
        out_shape=jax.ShapeDtypeStruct((width, hid), F32),
        grid=(width // strip,),
        in_specs=[
            pl.BlockSpec((total, strip), lambda i: (0, i)),
            pl.BlockSpec((total, hid), lambda i: (0, 0)),
            pl.BlockSpec((strip, hid), lambda i: (i, 0)),
        ],
        out_specs=pl.BlockSpec((strip, hid), lambda i: (i, 0)),
        compiler_params=pltpu.CompilerParams(vmem_limit_bytes=40 * 1024 * 1024),
        name="finish",
    )(every, mix, grad)
    return vector, score[0, 0:1]


def solution(mesh):
    placed = (
        P(("fsdp", "dp"), None),
        P(("fsdp", "dp"), None),
        P(None, ("fsdp", "dp"), None, None),
        P(("fsdp", "dp")),
        P(("fsdp", "dp")),
        P(None, "fsdp"),
        P("fsdp", None),
        P(None, "fsdp"),
    )
    return jax.shard_map(
        functools.partial(shards, mesh.shape["fsdp"], mesh.shape["dp"]),
        mesh=mesh,
        in_specs=placed,
        out_specs=(P(None, "fsdp"), P(("fsdp", "dp"))),
        check_vma=False,
    )
```

```python
import functools
import math

import jax
import jax.numpy as jnp
from jax import lax
from jax.experimental import pallas as pl
from jax.experimental.pallas import tpu as pltpu
from jax.sharding import PartitionSpec as P

STEPS_T = 10
CORES = 2

epsilon = 1e-06
sharpness_divisor = 6.0
keep = 1.0 - 0.01

BF = jnp.bfloat16
F32 = jnp.float32
MESH = pl.DeviceIdType.MESH


def dot32(a, b):
    return jnp.dot(a, b, preferred_element_type=F32)


def dot_t(a, b):
    return lax.dot_general(a, b, (((1,), (1,)), ((), ())), preferred_element_type=F32)


def loop(count, body):
    if count == 1:
        body(0)
    else:
        pl.loop(0, count)(body)


def tile(i, size):
    return pl.ds(pl.multiple_of(i * size, size), size)


def attend(noise, action, kv, flow):
    acts, width = noise.shape
    span = kv.shape[3]
    heads = width // span
    time = (flow[0].astype(F32) + 1.0) / (STEPS_T + 1.0)
    noisy = noise[...].astype(F32)
    clean = action[...].astype(F32)
    inputs = time * noisy + (1.0 - time) * clean
    queries = jnp.concatenate([inputs[:, h * span : (h + 1) * span] for h in range(heads)], 0)
    queries = queries * lax.rsqrt(jnp.mean(queries * queries, -1, keepdims=True) + epsilon)
    keys = kv[0, 0].astype(F32)
    keys = keys * lax.rsqrt(jnp.mean(keys * keys, -1, keepdims=True) + epsilon)
    expo = jnp.exp(dot_t(queries.astype(BF), keys.astype(BF)) * (sharpness_divisor / span))
    weights = (expo / jnp.sum(expo, -1, keepdims=True)).astype(BF)
    mixed = dot32(weights, kv[1, 0])
    mixed = jnp.concatenate([mixed[h * acts : (h + 1) * acts] for h in range(heads)], 1)
    hidden = inputs + mixed
    normed = hidden * lax.rsqrt(jnp.mean(hidden * hidden, -1, keepdims=True) + epsilon)
    return normed.astype(BF), hidden - (noisy - clean)


def kernel(
    nf, nd,
    noise, action, kv, flow, mask, w_up_h, w_down_h, grad_h,
    every_o, mix_o, score,
    w_up, w_down, grad, every, seconds0, seconds1, gram,
    slopes, curves, pulled, tan0, tan1, lhs, part, land0, land1, pair0, pair1,
    resid, tally, tally_in,
    load_sem, store_sem, f_send, f_recv, z_send, z_recv, c_send, c_recv,
):
    acts, width = noise.shape
    hid = w_up.shape[1]
    rows = nf * acts
    total = nd * rows
    chips = nd // CORES
    f = lax.axis_index("fsdp")
    d = lax.axis_index("dp")
    chip, core = d // CORES, d % CORES
    sibling = chip * CORES + (1 - core)

    def f_peer(k):
        return lax.rem(f + k, nf)

    def d_peer(k):
        return lax.rem(chip + k, chips) * CORES + core

    def d_from(k):
        return lax.rem(chip + chips - k, chips) * CORES + core

    barrier = pltpu.get_barrier_semaphore()
    for k in range(1, nf):
        pl.semaphore_signal(barrier, inc=1, device_id=(f_peer(k), d), device_id_type=MESH)
    for k in range(1, chips):
        pl.semaphore_signal(barrier, inc=1, device_id=(f, d_peer(k)), device_id_type=MESH)
    pl.semaphore_signal(barrier, inc=1, device_id=(f, sibling), device_id_type=MESH)

    loads = [
        pltpu.make_async_copy(src, dst, load_sem.at[i])
        for i, (src, dst) in enumerate(((w_up_h, w_up), (grad_h, grad), (w_down_h, w_down)))
    ]
    for load in loads:
        load.start()

    def remote(src, dst, send, recv, who):
        copy = pltpu.make_async_remote_copy(
            src_ref=src, dst_ref=dst, send_sem=send, recv_sem=recv, device_id=who, device_id_type=MESH
        )
        copy.start()
        return copy

    sent = []

    def fsdp(phase, src, dst):
        copies = [
            remote(src(f_peer(k)), dst(k), f_send.at[phase, k], f_recv.at[phase, k], (f_peer(k), d))
            for k in range(1, nf)
        ]
        if phase not in (1, 2):
            sent.extend(copies)
        return copies

    def landed(copies):
        for copy in copies:
            copy.wait_recv()

    def dp_start(phase, buf):
        mine = buf.at[tile(d, rows), :]
        z = [
            remote(mine, mine, z_send.at[phase, k], z_recv.at[phase, k], (f, d_peer(k)))
            for k in range(1, chips)
        ]
        c = [remote(mine, mine, c_send.at[phase, 0], c_recv.at[phase, 0], (f, sibling))]
        sent.extend(z)
        sent.extend(c)
        return z, c

    def dp_forward(phase, buf, z, c):
        for k in range(1, chips):
            z[k - 1].wait_recv()
            block = buf.at[tile(d_from(k), rows), :]
            copy = remote(block, block, c_send.at[phase, k], c_recv.at[phase, k], (f, sibling))
            sent.append(copy)
            c.append(copy)

    normed, left = attend(noise, action, kv, flow)
    resid[...] = left
    own = pl.ds(pl.multiple_of(d * rows + f * acts, acts), acts)
    every[own, :] = normed
    lane = lax.broadcasted_iota(jnp.int32, (acts, acts), 1)
    line = lax.broadcasted_iota(jnp.int32, (acts, acts), 0)
    valid = jnp.sum(
        jnp.where(lane == line, jnp.broadcast_to(mask[...].astype(F32), (acts, acts)), 0.0), -1, keepdims=True
    )
    pl.semaphore_wait(barrier, nf - 1 + chips)

    mine = every.at[own, :]
    landed(fsdp(0, lambda p: mine, lambda k: mine))
    group_at = tile(d, rows)
    z_n, c_n = dp_start(0, every)

    loads[0].wait()
    loads[1].wait()
    step = min(256, hid)

    def first(i):
        cut = tile(i, step)
        group = every[group_at, :]
        pre = dot32(group, w_up[:, cut])
        tangent = dot32(group, grad[:, cut].astype(BF))
        sig = 1.0 / (1.0 + jnp.exp(-pre))
        slope = sig * (1.0 + pre * (1.0 - sig))
        slopes[:, cut] = slope
        curves[:, cut] = sig * (1.0 - sig) * (2.0 + pre * (1.0 - 2.0 * sig))
        tan0[:, cut] = tangent
        lhs[0:rows, cut] = (pre * sig).astype(BF)
        lhs[rows : 2 * rows, cut] = (slope * tangent).astype(BF)

    loop(hid // step, first)
    loads[2].wait()
    wide = min(256, width)

    def down(i):
        cut = tile(i, wide)
        part[:, cut] = dot32(lhs[...], w_down[:, cut]).astype(BF)

    loop(width // wide, down)

    def rows_of(p, q):
        return pl.ds(pl.multiple_of(q * rows + p * acts, acts), acts)

    outs = fsdp(1, lambda p: part.at[rows_of(p, 0), :], lambda k: land0.at[k, 0:acts, :])
    moves = fsdp(2, lambda p: part.at[rows_of(p, 1), :], lambda k: land0.at[k, acts : 2 * acts, :])

    def summed(copies, q, land, lo):
        value = part[rows_of(f, q), :].astype(F32)
        for k in range(1, nf):
            copies[k - 1].wait_recv()
            value = value + land[k, lo : lo + acts, :].astype(F32)
        return value

    err = (valid * (resid[...] + summed(outs, 0, land0, 0))).astype(BF)
    pair0[rows_of(f, 0), :] = err
    errs = fsdp(3, lambda p: pair0.at[rows_of(f, 0), :], lambda k: pair0.at[rows_of(f, 0), :])
    pair0[rows_of(f, 1), :] = (valid * summed(moves, 1, land0, acts)).astype(BF)
    merrs = fsdp(4, lambda p: pair0.at[rows_of(f, 1), :], lambda k: pair0.at[rows_of(f, 1), :])
    dp_forward(0, every, z_n, c_n)
    landed(errs)
    landed(merrs)

    def bend(i):
        cut = tile(i, step)
        both = dot_t(pair0[...], w_down[cut, :])
        pull = both[0:rows]
        pulled[:, cut] = pull
        seconds0[group_at, cut] = (
            both[rows : 2 * rows] * slopes[:, cut] + pull * curves[:, cut] * tan0[:, cut]
        ).astype(BF)

    loop(hid // step, bend)
    z_0, c_0 = dp_start(1, seconds0)
    landed(c_n)
    keep_every = pltpu.make_async_copy(every, every_o, store_sem.at[0])
    keep_every.start()
    chunk = min(512, total)

    def grams(i):
        cut = tile(i, chunk)
        gram[:, cut] = (dot_t(every[group_at, :], every[cut, :]) / total).astype(BF)

    loop(total // chunk, grams)
    dp_forward(1, seconds0, z_0, c_0)
    landed(c_0)

    def fold(seconds, cut):
        if total == chunk:
            return dot32(gram[...], seconds[:, cut])
        return lax.fori_loop(
            0,
            total // chunk,
            lambda j, v: v + dot32(gram[:, tile(j, chunk)], seconds[tile(j, chunk), cut]),
            jnp.zeros((rows, step), F32),
        )

    def again(i):
        cut = tile(i, step)
        tangent = (1.0 + keep) * tan0[:, cut] - fold(seconds0, cut)
        tan1[:, cut] = tangent
        lhs[0:rows, cut] = (slopes[:, cut] * tangent).astype(BF)

    loop(hid // step, again)
    for copy in outs + moves:
        copy.wait_send()

    def down_again(i):
        cut = tile(i, wide)
        part[0:rows, cut] = dot32(lhs[0:rows, :], w_down[:, cut]).astype(BF)

    loop(width // wide, down_again)
    moves1 = fsdp(5, lambda p: part.at[rows_of(p, 0), :], lambda k: land1.at[k])
    pair1[rows_of(f, 0), :] = (valid * summed(moves1, 0, land1, 0)).astype(BF)
    landed(fsdp(6, lambda p: pair1.at[rows_of(f, 0), :], lambda k: pair1.at[rows_of(f, 0), :]))

    def bend_again(i):
        cut = tile(i, step)
        both = dot_t(pair1[...], w_down[cut, :])
        seconds1[group_at, cut] = (
            both * slopes[:, cut] + pulled[:, cut] * curves[:, cut] * tan1[:, cut]
        ).astype(BF)

    loop(hid // step, bend_again)
    z_1, c_1 = dp_start(2, seconds1)
    dp_forward(2, seconds1, z_1, c_1)
    landed(c_1)
    for copy in sent:
        copy.wait_send()

    def blend(i):
        cut = tile(i, rows)
        seconds1[cut, :] = (
            keep * seconds0[cut, :].astype(F32) + seconds1[cut, :].astype(F32)
        ).astype(BF)

    loop(nd, blend)
    keep_mix = pltpu.make_async_copy(seconds1, mix_o, store_sem.at[1])
    keep_mix.start()
    scale = 1.0 + keep + keep * keep

    def rate(i, terms):
        cut = tile(i, step)
        projected = scale * tan0[:, cut] - fold(seconds1, cut)
        return terms + projected * (pulled[:, cut] * slopes[:, cut])

    terms = lax.fori_loop(0, hid // step, rate, jnp.zeros((rows, step), F32))
    for p in range(nf):
        one = jnp.sum(terms[p * acts : (p + 1) * acts], 0, keepdims=True)
        tally[p] = jnp.broadcast_to(jnp.sum(one, -1, keepdims=True), tally.shape[1:])
    votes = [
        remote(tally.at[f_peer(k)], tally_in.at[k], f_send.at[7, k], f_recv.at[7, k], (f_peer(k), d))
        for k in range(1, nf)
    ]
    value = tally[f]
    for k in range(1, nf):
        votes[k - 1].wait_recv()
        value = value + tally_in[k]
    score[...] = -value / (acts * math.sqrt(width * hid * nf))
    for copy in votes:
        copy.wait_send()
    keep_every.wait()
    keep_mix.wait()


def spread(
    nf, nd,
    noise_h, action_h, kv_h, flow, mask_h, w_up_h, w_down_h, grad_h,
    out, score,
    noise, action, kv, mask, w_up, w_down, grad, gradb, every, flipped, seconds, gram,
    slopes, curves, pulled, tan0, tan1, lhs, part, land0, land1, pair0, pair1,
    resid, tally, tally_in,
    load_sem, store_sem, f_send, f_recv, z_send, z_recv, x_send, x_recv, c_send, c_recv,
):
    acts, width = noise.shape
    hid = w_up.shape[1]
    rows = nf * acts
    total = nd * rows
    chips = nd // CORES
    pack = chips * rows
    step = min(256, hid)
    wide = min(256, width)
    f = lax.axis_index("fsdp")
    d = lax.axis_index("dp")
    chip, core = d // CORES, d % CORES
    sibling = chip * CORES + (1 - core)

    def f_peer(k):
        return lax.rem(f + k, nf)

    def f_from(k):
        return lax.rem(f + nf - k, nf)

    def d_peer(k):
        return lax.rem(chip + k, chips) * CORES + core

    def chip_from(k):
        return lax.rem(chip + chips - k, chips)

    barrier = pltpu.get_barrier_semaphore()
    for k in range(1, nf):
        pl.semaphore_signal(barrier, inc=1, device_id=(f_peer(k), d), device_id_type=MESH)
    for k in range(1, chips):
        pl.semaphore_signal(barrier, inc=1, device_id=(f, d_peer(k)), device_id_type=MESH)
    pl.semaphore_signal(barrier, inc=1, device_id=(f, sibling), device_id_type=MESH)

    pairs = (
        (noise_h, noise), (action_h, action), (kv_h, kv), (mask_h, mask),
        (w_up_h, w_up), (grad_h, grad), (w_down_h, w_down),
    )
    loads = [pltpu.make_async_copy(src, dst, load_sem.at[i]) for i, (src, dst) in enumerate(pairs)]
    for load in loads:
        load.start()

    def remote(src, dst, send, recv, who):
        copy = pltpu.make_async_remote_copy(
            src_ref=src, dst_ref=dst, send_sem=send, recv_sem=recv, device_id=who, device_id_type=MESH
        )
        copy.start()
        return copy

    sent = []

    def scatter(phase, src, dst):
        return [
            remote(src(f_peer(k)), dst(k), f_send.at[phase, k], f_recv.at[phase, k], (f_peer(k), d))
            for k in range(1, nf)
        ]

    def block(g, kk, k):
        who = chip_from(kk)
        if g == 1:
            return pair0.at[who, :, tile(f_from(k), acts), :]
        if g == 0:
            who = core * chips + who
        at = pl.ds(pl.multiple_of(who * rows + f_from(k) * acts, acts), acts)
        return (every if g == 0 else pair1).at[at, :]

    across, to_core, along = {}, {}, {}

    def keep_copy(table, key, copy):
        table[key] = copy
        sent.append(copy)

    def share(g, kk):
        mine = block(g, kk, 0)
        for k in range(1, nf):
            keep_copy(across, (g, kk, k), remote(
                mine, mine, x_send.at[g, kk, k], x_recv.at[g, kk, k], (f_peer(k), d)
            ))

    def begin(g):
        mine = block(g, 0, 0)
        for k in range(1, chips):
            keep_copy(along, (g, k), remote(
                mine, mine, z_send.at[g, k], z_recv.at[g, k], (f, d_peer(k))
            ))
        share(g, 0)

    def from_z(g):
        for kk in range(1, chips):
            along[g, kk].wait_recv()
            share(g, kk)

    def from_f(g, kk):
        for k in range(1, nf):
            across[g, kk, k].wait_recv()

    def swap(g, kk):
        at = tile(core * chips + chip_from(kk), rows)
        mine = every.at[at, :] if g == 0 else seconds.at[g - 1, at, :]
        keep_copy(to_core, (g, kk), remote(
            mine, mine, c_send.at[g, kk], c_recv.at[g, kk], (f, sibling)
        ))

    def swapped(g):
        for kk in range(chips):
            to_core[g, kk].wait_recv()

    for load in loads[:4]:
        load.wait()
    normed, left = attend(noise, action, kv, flow)
    resid[...] = left
    own = pl.ds(pl.multiple_of((core * chips + chip) * rows + f * acts, acts), acts)
    every[own, :] = normed
    lane = lax.broadcasted_iota(jnp.int32, (acts, acts), 1)
    line = lax.broadcasted_iota(jnp.int32, (acts, acts), 0)
    valid = jnp.sum(
        jnp.where(lane == line, jnp.broadcast_to(mask[...].astype(F32), (acts, acts)), 0.0), -1, keepdims=True
    )
    pl.semaphore_wait(barrier, nf - 1 + chips)
    begin(0)
    group_at = tile(chip, rows)

    def first(whole, at, cut):
        group = every[whole, :]
        pre = dot32(group, w_up[:, cut])
        tangent = dot32(group, gradb[:, cut])
        sig = 1.0 / (1.0 + jnp.exp(-pre))
        slope = sig * (1.0 + pre * (1.0 - sig))
        slopes[at, cut] = slope
        curves[at, cut] = sig * (1.0 - sig) * (2.0 + pre * (1.0 - 2.0 * sig))
        tan0[at, cut] = tangent
        return pre * sig, slope * tangent

    def first_own(i):
        cut = tile(i, step)
        active, linear = first(tile(core * chips + chip, rows), group_at, cut)
        lhs[0:rows, cut] = active.astype(BF)
        lhs[rows : 2 * rows, cut] = linear.astype(BF)

    loads[5].wait()

    def narrow(i):
        cut = tile(i, wide)
        gradb[cut, :] = grad[cut, :].astype(BF)

    loop(width // wide, narrow)
    loads[4].wait()
    from_f(0, 0)
    swap(0, 0)
    first_own(0)
    from_z(0)
    if hid > step:
        pl.loop(1, hid // step)(first_own)
    loads[6].wait()

    def down(i):
        cut = tile(i, wide)
        part[:, cut] = dot32(lhs[...], w_down[:, cut]).astype(BF)

    loop(width // wide, down)

    def rows_of(p, q):
        return pl.ds(pl.multiple_of(q * rows + p * acts, acts), acts)

    outs = scatter(0, lambda p: part.at[rows_of(p, 0), :], lambda k: land0.at[k, 0:acts, :])
    moves = scatter(1, lambda p: part.at[rows_of(p, 1), :], lambda k: land0.at[k, acts : 2 * acts, :])

    def summed(copies, q, land, lo):
        value = part[rows_of(f, q), :].astype(F32)
        for k in range(1, nf):
            copies[k - 1].wait_recv()
            value = value + land[k, lo : lo + acts, :].astype(F32)
        return value

    here = tile(f, acts)
    pair0[chip, 0, here, :] = (valid * (resid[...] + summed(outs, 0, land0, 0))).astype(BF)
    pair0[chip, 1, here, :] = (valid * summed(moves, 1, land0, acts)).astype(BF)
    begin(1)
    for kk in range(1, chips):
        from_f(0, kk)
        swap(0, kk)

    def rest(i):
        first(tile(core, pack), slice(None), tile(i, step))

    rest(0)
    from_z(1)
    if hid > step:
        pl.loop(1, hid // step)(rest)
    swapped(0)

    def grams(i):
        cut = tile(i, pack)
        gram[:, cut] = (dot_t(every[tile(core, pack), :], every[cut, :]) * (1.0 / total)).astype(BF)

    loop(CORES, grams)

    def flip(i):
        cut = tile(i, wide)
        flipped[cut, :] = every[:, cut].T

    loop(width // wide, flip)

    def bend(kk):
        at = tile(chip_from(kk), rows)
        whole = tile(core * chips + chip_from(kk), rows)

        def body(i):
            cut = tile(i, step)
            both = dot_t(pair0[chip_from(kk)].reshape(2 * rows, width), w_down[cut, :])
            pull = both[0:rows]
            pulled[at, cut] = pull
            seconds[0, whole, cut] = (
                both[rows : 2 * rows] * slopes[at, cut] + pull * curves[at, cut] * tan0[at, cut]
            ).astype(BF)

        loop(hid // step, body)

    for kk in range(chips):
        from_f(1, kk)
        bend(kk)
        swap(1, kk)
    swapped(1)

    def again(at, cut):
        tangent = (1.0 + keep) * tan0[at, cut] - dot32(gram[at, :], seconds[0, :, cut])
        tan1[at, cut] = tangent
        return tangent

    def again_own(i):
        cut = tile(i, step)
        lhs[0:rows, cut] = (slopes[group_at, cut] * again(group_at, cut)).astype(BF)

    loop(hid // step, again_own)
    for copy in outs + moves:
        copy.wait_send()

    def down_again(i):
        cut = tile(i, wide)
        part[0:rows, cut] = dot32(lhs[0:rows, :], w_down[:, cut]).astype(BF)

    loop(width // wide, down_again)
    moves1 = scatter(2, lambda p: part.at[rows_of(p, 0), :], lambda k: land1.at[k])
    sent.extend(moves1)

    def again_all(i):
        again(slice(None), tile(i, step))

    loop(hid // step, again_all)
    pair1[pl.ds(pl.multiple_of(chip * rows + f * acts, acts), acts), :] = (valid * summed(moves1, 0, land1, 0)).astype(BF)
    begin(2)

    def settle(i):
        cut = tile(i, wide)
        change = dot32(flipped[cut, :], seconds[0])
        grad[cut, :] = (1.0 + keep + keep * keep) * grad[cut, :] - (keep / total) * change

    half = max(1, width // wide // 2)
    pl.loop(0, half)(settle)
    from_z(2)
    pl.loop(half, width // wide)(settle)

    def bend_again(kk):
        at = tile(chip_from(kk), rows)
        whole = tile(core * chips + chip_from(kk), rows)

        def body(i):
            cut = tile(i, step)
            both = dot_t(pair1[at, :], w_down[cut, :])
            seconds[1, whole, cut] = (
                both * slopes[at, cut] + pulled[at, cut] * curves[at, cut] * tan1[at, cut]
            ).astype(BF)

        loop(hid // step, body)

    for kk in range(chips):
        from_f(2, kk)
        bend_again(kk)
        swap(2, kk)
    swapped(2)

    def rate(i, terms):
        cut = tile(i, step)
        projected = tan0[group_at, cut] + keep * tan1[group_at, cut]
        projected = projected - dot32(gram[group_at, :], seconds[1, :, cut])
        return terms + projected * (pulled[group_at, cut] * slopes[group_at, cut])

    terms = lax.fori_loop(0, hid // step, rate, jnp.zeros((rows, step), F32))
    for p in range(nf):
        one = jnp.sum(terms[p * acts : (p + 1) * acts], 0, keepdims=True)
        tally[p] = jnp.broadcast_to(jnp.sum(one, -1, keepdims=True), tally.shape[1:])
    votes = scatter(3, lambda p: tally.at[p], lambda k: tally_in.at[k])
    sent.extend(votes)
    stores = []
    for i in range(width // wide):
        cut = pl.ds(i * wide, wide)
        grad[cut, :] = grad[cut, :] - dot32(flipped[cut, :], seconds[1]) * (1.0 / total)
        stores.append(pltpu.make_async_copy(grad.at[cut, :], out.at[cut, :], store_sem.at[i]))
        stores[-1].start()
    value = tally[f]
    for k in range(1, nf):
        votes[k - 1].wait_recv()
        value = value + tally_in[k]
    score[...] = -value / (acts * math.sqrt(width * hid * nf))
    for copy in sent:
        copy.wait_send()
    for store in stores:
        store.wait()


def hand_out(held, tally, out, score, stage, sems):
    parts = sems.shape[1]
    high = out.shape[0] // parts

    def move(i, to):
        at = pl.ds(i * high, high)
        src, dst = (stage, out) if to else (held, stage)
        return pltpu.make_async_copy(src.at[at, :], dst.at[at, :], sems.at[to, i])

    loads = [move(i, 0) for i in range(parts)]
    stores = [move(i, 1) for i in range(parts)]
    for load in loads:
        load.start()
    score[0] = tally[0, 0]
    for load, store in zip(loads, stores):
        load.wait()
        store.start()
    for store in stores:
        store.wait()


def spread_call(nf, nd, noise, action, kv, flow, mask, w_up, w_down, grad):
    acts, width = noise.shape
    hid = w_up.shape[1]
    rows = nf * acts
    total = nd * rows
    chips = nd // CORES
    vmem = pl.BlockSpec(memory_space=pltpu.VMEM)
    anywhere = pl.BlockSpec(memory_space=pl.ANY)
    dma = pltpu.SemaphoreType.DMA
    half, full = (lambda *s: pltpu.VMEM(s, BF)), (lambda *s: pltpu.VMEM(s, F32))
    vector, score = pl.pallas_call(
        functools.partial(spread, nf, nd),
        out_shape=(jax.ShapeDtypeStruct((width, hid), F32), jax.ShapeDtypeStruct((8, 128), F32)),
        in_specs=[anywhere] * 3 + [pl.BlockSpec(memory_space=pltpu.SMEM)] + [anywhere] * 4,
        out_specs=(anywhere, vmem),
        scratch_shapes=[
            half(acts, width), half(acts, width), half(*kv.shape), pltpu.VMEM((1, acts), jnp.int32),
            half(width, hid), half(hid, width), full(width, hid), half(width, hid),
            half(total, width), half(width, total), half(2, total, hid), half(total // CORES, total),
        ] + [full(total // CORES, hid)] * 5 + [
            half(2 * rows, hid), half(2 * rows, width), half(nf, 2 * acts, width), half(nf, acts, width),
            half(chips, 2, rows, width), half(total // CORES, width),
            full(acts, width), full(nf, 8, 128), full(nf, 8, 128),
            dma((7,)), dma((max(1, width // 256),)), dma((4, nf)), dma((4, nf)),
            dma((3, chips)), dma((3, chips)), dma((3, chips, nf)), dma((3, chips, nf)),
            dma((3, chips)), dma((3, chips)),
        ],
        compiler_params=pltpu.CompilerParams(
            collective_id=0, has_side_effects=True, vmem_limit_bytes=60 * 1024 * 1024
        ),
        name="lissa",
    )(noise, action, kv, flow, mask.reshape(1, acts), w_up, w_down, grad)
    return pl.pallas_call(
        hand_out,
        out_shape=(jax.ShapeDtypeStruct((width, hid), F32), jax.ShapeDtypeStruct((1,), F32)),
        in_specs=[anywhere, vmem],
        out_specs=(anywhere, pl.BlockSpec(memory_space=pltpu.SMEM)),
        scratch_shapes=[full(width, hid), dma((2, 8))],
        compiler_params=pltpu.CompilerParams(vmem_limit_bytes=60 * 1024 * 1024),
        name="hand_out",
    )(vector, score)


def finish(total, every, mix, grad, out):
    change = lax.dot_general(
        every[...], mix[...], (((0,), (0,)), ((), ())), preferred_element_type=F32
    )
    out[...] = (1.0 + keep + keep * keep) * grad[...] - change / total


def shards(nf, nd, noise, action, kv, flow, mask, w_up, w_down, grad):
    acts, width = noise.shape
    hid = w_up.shape[1]
    rows = nf * acts
    total = nd * rows
    if total <= 512:
        return spread_call(nf, nd, noise, action, kv, flow, mask, w_up, w_down, grad)
    vmem = pl.BlockSpec(memory_space=pltpu.VMEM)
    anywhere = pl.BlockSpec(memory_space=pl.ANY)
    dma = pltpu.SemaphoreType.DMA
    chips = nd // CORES
    every, mix, score = pl.pallas_call(
        functools.partial(kernel, nf, nd),
        out_shape=(
            jax.ShapeDtypeStruct((total, width), BF),
            jax.ShapeDtypeStruct((total, hid), BF),
            jax.ShapeDtypeStruct((8, 128), F32),
        ),
        in_specs=[
            vmem, vmem, vmem, pl.BlockSpec(memory_space=pltpu.SMEM), vmem, anywhere, anywhere, anywhere,
        ],
        out_specs=(anywhere, anywhere, vmem),
        scratch_shapes=[
            pltpu.VMEM((width, hid), BF),
            pltpu.VMEM((hid, width), BF),
            pltpu.VMEM((width, hid), F32),
            pltpu.VMEM((total, width), BF),
            pltpu.VMEM((total, hid), BF),
            pltpu.VMEM((total, hid), BF),
            pltpu.VMEM((rows, total), BF),
            pltpu.VMEM((rows, hid), F32),
            pltpu.VMEM((rows, hid), F32),
            pltpu.VMEM((rows, hid), F32),
            pltpu.VMEM((rows, hid), F32),
            pltpu.VMEM((rows, hid), F32),
            pltpu.VMEM((2 * rows, hid), BF),
            pltpu.VMEM((2 * rows, width), BF),
            pltpu.VMEM((nf, 2 * acts, width), BF),
            pltpu.VMEM((nf, acts, width), BF),
            pltpu.VMEM((2 * rows, width), BF),
            pltpu.VMEM((rows, width), BF),
            pltpu.VMEM((acts, width), F32),
            pltpu.VMEM((nf, 8, 128), F32),
            pltpu.VMEM((nf, 8, 128), F32),
            dma((3,)),
            dma((2,)),
            dma((8, nf)),
            dma((8, nf)),
            dma((3, chips)),
            dma((3, chips)),
            dma((3, chips)),
            dma((3, chips)),
        ],
        compiler_params=pltpu.CompilerParams(
            collective_id=0, has_side_effects=True, vmem_limit_bytes=52 * 1024 * 1024
        ),
        name="lissa",
    )(noise, action, kv, flow, mask.reshape(1, acts), w_up, w_down, grad)
    strip = 128
    vector = pl.pallas_call(
        functools.partial(finish, total),
        out_shape=jax.ShapeDtypeStruct((width, hid), F32),
        grid=(width // strip,),
        in_specs=[
            pl.BlockSpec((total, strip), lambda i: (0, i)),
            pl.BlockSpec((total, hid), lambda i: (0, 0)),
            pl.BlockSpec((strip, hid), lambda i: (i, 0)),
        ],
        out_specs=pl.BlockSpec((strip, hid), lambda i: (i, 0)),
        compiler_params=pltpu.CompilerParams(vmem_limit_bytes=40 * 1024 * 1024),
        name="finish",
    )(every, mix, grad)
    return vector, score[0, 0:1]


def solution(mesh):
    placed = (
        P(("fsdp", "dp"), None),
        P(("fsdp", "dp"), None),
        P(None, ("fsdp", "dp"), None, None),
        P(("fsdp", "dp")),
        P(("fsdp", "dp")),
        P(None, "fsdp"),
        P("fsdp", None),
        P(None, "fsdp"),
    )
    return jax.shard_map(
        functools.partial(shards, mesh.shape["fsdp"], mesh.shape["dp"]),
        mesh=mesh,
        in_specs=placed,
        out_specs=(P(None, "fsdp"), P(("fsdp", "dp"))),
        check_vma=False,
    )
```

```python
import functools
import math

import jax
import jax.numpy as jnp
from jax import lax
from jax.experimental import pallas as pl
from jax.experimental.pallas import tpu as pltpu
from jax.sharding import PartitionSpec as P

STEPS_T = 10
CORES = 2

epsilon = 1e-06
sharpness_divisor = 6.0
keep = 1.0 - 0.01

BF = jnp.bfloat16
F32 = jnp.float32
MESH = pl.DeviceIdType.MESH


def dot32(a, b):
    return jnp.dot(a, b, preferred_element_type=F32)


def dot_t(a, b):
    return lax.dot_general(a, b, (((1,), (1,)), ((), ())), preferred_element_type=F32)


def loop(count, body):
    if count == 1:
        body(0)
    else:
        pl.loop(0, count)(body)


def tile(i, size):
    return pl.ds(pl.multiple_of(i * size, size), size)


def attend(noise, action, kv, flow):
    acts, width = noise.shape
    span = kv.shape[3]
    heads = width // span
    time = (flow[0].astype(F32) + 1.0) / (STEPS_T + 1.0)
    noisy = noise[...].astype(F32)
    clean = action[...].astype(F32)
    inputs = time * noisy + (1.0 - time) * clean
    queries = jnp.concatenate([inputs[:, h * span : (h + 1) * span] for h in range(heads)], 0)
    queries = queries * lax.rsqrt(jnp.mean(queries * queries, -1, keepdims=True) + epsilon)
    keys = kv[0, 0].astype(F32)
    keys = keys * lax.rsqrt(jnp.mean(keys * keys, -1, keepdims=True) + epsilon)
    expo = jnp.exp(dot_t(queries.astype(BF), keys.astype(BF)) * (sharpness_divisor / span))
    weights = (expo / jnp.sum(expo, -1, keepdims=True)).astype(BF)
    mixed = dot32(weights, kv[1, 0])
    mixed = jnp.concatenate([mixed[h * acts : (h + 1) * acts] for h in range(heads)], 1)
    hidden = inputs + mixed
    normed = hidden * lax.rsqrt(jnp.mean(hidden * hidden, -1, keepdims=True) + epsilon)
    return normed.astype(BF), hidden - (noisy - clean)


def kernel(
    nf, nd,
    noise, action, kv, flow, mask, w_up_h, w_down_h, grad_h,
    every_o, mix_o, score,
    w_up, w_down, grad, every, seconds0, seconds1, gram,
    slopes, curves, pulled, tan0, tan1, lhs, part, land0, land1, pair0, pair1,
    resid, tally, tally_in,
    load_sem, store_sem, f_send, f_recv, z_send, z_recv, c_send, c_recv,
):
    acts, width = noise.shape
    hid = w_up.shape[1]
    rows = nf * acts
    total = nd * rows
    chips = nd // CORES
    f = lax.axis_index("fsdp")
    d = lax.axis_index("dp")
    chip, core = d // CORES, d % CORES
    sibling = chip * CORES + (1 - core)

    def f_peer(k):
        return lax.rem(f + k, nf)

    def d_peer(k):
        return lax.rem(chip + k, chips) * CORES + core

    def d_from(k):
        return lax.rem(chip + chips - k, chips) * CORES + core

    barrier = pltpu.get_barrier_semaphore()
    for k in range(1, nf):
        pl.semaphore_signal(barrier, inc=1, device_id=(f_peer(k), d), device_id_type=MESH)
    for k in range(1, chips):
        pl.semaphore_signal(barrier, inc=1, device_id=(f, d_peer(k)), device_id_type=MESH)
    pl.semaphore_signal(barrier, inc=1, device_id=(f, sibling), device_id_type=MESH)

    loads = [
        pltpu.make_async_copy(src, dst, load_sem.at[i])
        for i, (src, dst) in enumerate(((w_up_h, w_up), (grad_h, grad), (w_down_h, w_down)))
    ]
    for load in loads:
        load.start()

    def remote(src, dst, send, recv, who):
        copy = pltpu.make_async_remote_copy(
            src_ref=src, dst_ref=dst, send_sem=send, recv_sem=recv, device_id=who, device_id_type=MESH
        )
        copy.start()
        return copy

    sent = []

    def fsdp(phase, src, dst):
        copies = [
            remote(src(f_peer(k)), dst(k), f_send.at[phase, k], f_recv.at[phase, k], (f_peer(k), d))
            for k in range(1, nf)
        ]
        if phase not in (1, 2):
            sent.extend(copies)
        return copies

    def landed(copies):
        for copy in copies:
            copy.wait_recv()

    def dp_start(phase, buf):
        mine = buf.at[tile(d, rows), :]
        z = [
            remote(mine, mine, z_send.at[phase, k], z_recv.at[phase, k], (f, d_peer(k)))
            for k in range(1, chips)
        ]
        c = [remote(mine, mine, c_send.at[phase, 0], c_recv.at[phase, 0], (f, sibling))]
        sent.extend(z)
        sent.extend(c)
        return z, c

    def dp_forward(phase, buf, z, c):
        for k in range(1, chips):
            z[k - 1].wait_recv()
            block = buf.at[tile(d_from(k), rows), :]
            copy = remote(block, block, c_send.at[phase, k], c_recv.at[phase, k], (f, sibling))
            sent.append(copy)
            c.append(copy)

    normed, left = attend(noise, action, kv, flow)
    resid[...] = left
    own = pl.ds(pl.multiple_of(d * rows + f * acts, acts), acts)
    every[own, :] = normed
    lane = lax.broadcasted_iota(jnp.int32, (acts, acts), 1)
    line = lax.broadcasted_iota(jnp.int32, (acts, acts), 0)
    valid = jnp.sum(
        jnp.where(lane == line, jnp.broadcast_to(mask[...].astype(F32), (acts, acts)), 0.0), -1, keepdims=True
    )
    pl.semaphore_wait(barrier, nf - 1 + chips)

    mine = every.at[own, :]
    landed(fsdp(0, lambda p: mine, lambda k: mine))
    group_at = tile(d, rows)
    z_n, c_n = dp_start(0, every)

    loads[0].wait()
    loads[1].wait()
    step = min(256, hid)

    def first(i):
        cut = tile(i, step)
        group = every[group_at, :]
        pre = dot32(group, w_up[:, cut])
        tangent = dot32(group, grad[:, cut].astype(BF))
        sig = 1.0 / (1.0 + jnp.exp(-pre))
        slope = sig * (1.0 + pre * (1.0 - sig))
        slopes[:, cut] = slope
        curves[:, cut] = sig * (1.0 - sig) * (2.0 + pre * (1.0 - 2.0 * sig))
        tan0[:, cut] = tangent
        lhs[0:rows, cut] = (pre * sig).astype(BF)
        lhs[rows : 2 * rows, cut] = (slope * tangent).astype(BF)

    loop(hid // step, first)
    loads[2].wait()
    wide = min(256, width)

    def down(i):
        cut = tile(i, wide)
        part[:, cut] = dot32(lhs[...], w_down[:, cut]).astype(BF)

    loop(width // wide, down)

    def rows_of(p, q):
        return pl.ds(pl.multiple_of(q * rows + p * acts, acts), acts)

    outs = fsdp(1, lambda p: part.at[rows_of(p, 0), :], lambda k: land0.at[k, 0:acts, :])
    moves = fsdp(2, lambda p: part.at[rows_of(p, 1), :], lambda k: land0.at[k, acts : 2 * acts, :])

    def summed(copies, q, land, lo):
        value = part[rows_of(f, q), :].astype(F32)
        for k in range(1, nf):
            copies[k - 1].wait_recv()
            value = value + land[k, lo : lo + acts, :].astype(F32)
        return value

    err = (valid * (resid[...] + summed(outs, 0, land0, 0))).astype(BF)
    pair0[rows_of(f, 0), :] = err
    errs = fsdp(3, lambda p: pair0.at[rows_of(f, 0), :], lambda k: pair0.at[rows_of(f, 0), :])
    pair0[rows_of(f, 1), :] = (valid * summed(moves, 1, land0, acts)).astype(BF)
    merrs = fsdp(4, lambda p: pair0.at[rows_of(f, 1), :], lambda k: pair0.at[rows_of(f, 1), :])
    dp_forward(0, every, z_n, c_n)
    landed(errs)
    landed(merrs)

    def bend(i):
        cut = tile(i, step)
        both = dot_t(pair0[...], w_down[cut, :])
        pull = both[0:rows]
        pulled[:, cut] = pull
        seconds0[group_at, cut] = (
            both[rows : 2 * rows] * slopes[:, cut] + pull * curves[:, cut] * tan0[:, cut]
        ).astype(BF)

    loop(hid // step, bend)
    z_0, c_0 = dp_start(1, seconds0)
    landed(c_n)
    keep_every = pltpu.make_async_copy(every, every_o, store_sem.at[0])
    keep_every.start()
    chunk = min(512, total)

    def grams(i):
        cut = tile(i, chunk)
        gram[:, cut] = (dot_t(every[group_at, :], every[cut, :]) / total).astype(BF)

    loop(total // chunk, grams)
    dp_forward(1, seconds0, z_0, c_0)
    landed(c_0)

    def fold(seconds, cut):
        if total == chunk:
            return dot32(gram[...], seconds[:, cut])
        return lax.fori_loop(
            0,
            total // chunk,
            lambda j, v: v + dot32(gram[:, tile(j, chunk)], seconds[tile(j, chunk), cut]),
            jnp.zeros((rows, step), F32),
        )

    def again(i):
        cut = tile(i, step)
        tangent = (1.0 + keep) * tan0[:, cut] - fold(seconds0, cut)
        tan1[:, cut] = tangent
        lhs[0:rows, cut] = (slopes[:, cut] * tangent).astype(BF)

    loop(hid // step, again)
    for copy in outs + moves:
        copy.wait_send()

    def down_again(i):
        cut = tile(i, wide)
        part[0:rows, cut] = dot32(lhs[0:rows, :], w_down[:, cut]).astype(BF)

    loop(width // wide, down_again)
    moves1 = fsdp(5, lambda p: part.at[rows_of(p, 0), :], lambda k: land1.at[k])
    pair1[rows_of(f, 0), :] = (valid * summed(moves1, 0, land1, 0)).astype(BF)
    landed(fsdp(6, lambda p: pair1.at[rows_of(f, 0), :], lambda k: pair1.at[rows_of(f, 0), :]))

    def bend_again(i):
        cut = tile(i, step)
        both = dot_t(pair1[...], w_down[cut, :])
        seconds1[group_at, cut] = (
            both * slopes[:, cut] + pulled[:, cut] * curves[:, cut] * tan1[:, cut]
        ).astype(BF)

    loop(hid // step, bend_again)
    z_1, c_1 = dp_start(2, seconds1)
    dp_forward(2, seconds1, z_1, c_1)
    landed(c_1)
    for copy in sent:
        copy.wait_send()

    def blend(i):
        cut = tile(i, rows)
        seconds1[cut, :] = (
            keep * seconds0[cut, :].astype(F32) + seconds1[cut, :].astype(F32)
        ).astype(BF)

    loop(nd, blend)
    keep_mix = pltpu.make_async_copy(seconds1, mix_o, store_sem.at[1])
    keep_mix.start()
    scale = 1.0 + keep + keep * keep

    def rate(i, terms):
        cut = tile(i, step)
        projected = scale * tan0[:, cut] - fold(seconds1, cut)
        return terms + projected * (pulled[:, cut] * slopes[:, cut])

    terms = lax.fori_loop(0, hid // step, rate, jnp.zeros((rows, step), F32))
    for p in range(nf):
        one = jnp.sum(terms[p * acts : (p + 1) * acts], 0, keepdims=True)
        tally[p] = jnp.broadcast_to(jnp.sum(one, -1, keepdims=True), tally.shape[1:])
    votes = [
        remote(tally.at[f_peer(k)], tally_in.at[k], f_send.at[7, k], f_recv.at[7, k], (f_peer(k), d))
        for k in range(1, nf)
    ]
    value = tally[f]
    for k in range(1, nf):
        votes[k - 1].wait_recv()
        value = value + tally_in[k]
    score[...] = -value / (acts * math.sqrt(width * hid * nf))
    for copy in votes:
        copy.wait_send()
    keep_every.wait()
    keep_mix.wait()


def spread(
    nf, nd,
    noise_h, action_h, kv_h, flow, mask_h, w_up_h, w_down_h, grad_h,
    out, score,
    noise, action, kv, mask, w_up, w_down, grad, gradb, every, flipped, seconds, gram,
    slopes, curves, pulled, tan0, tan1, lhs, part, land0, land1, pair0, pair1,
    resid, tally, tally_in,
    load_sem, store_sem, f_send, f_recv, z_send, z_recv, x_send, x_recv, c_send, c_recv,
):
    acts, width = noise.shape
    hid = w_up.shape[1]
    rows = nf * acts
    total = nd * rows
    chips = nd // CORES
    pack = chips * rows
    step = min(256, hid)
    wide = min(256, width)
    f = lax.axis_index("fsdp")
    d = lax.axis_index("dp")
    chip, core = d // CORES, d % CORES
    sibling = chip * CORES + (1 - core)

    def f_peer(k):
        return lax.rem(f + k, nf)

    def f_from(k):
        return lax.rem(f + nf - k, nf)

    def d_peer(k):
        return lax.rem(chip + k, chips) * CORES + core

    def chip_from(k):
        return lax.rem(chip + chips - k, chips)

    barrier = pltpu.get_barrier_semaphore()
    for k in range(1, nf):
        pl.semaphore_signal(barrier, inc=1, device_id=(f_peer(k), d), device_id_type=MESH)
    for k in range(1, chips):
        pl.semaphore_signal(barrier, inc=1, device_id=(f, d_peer(k)), device_id_type=MESH)
    pl.semaphore_signal(barrier, inc=1, device_id=(f, sibling), device_id_type=MESH)

    pairs = (
        (noise_h, noise), (action_h, action), (kv_h, kv), (mask_h, mask),
        (w_up_h, w_up), (grad_h, grad), (w_down_h, w_down),
    )
    loads = [pltpu.make_async_copy(src, dst, load_sem.at[i]) for i, (src, dst) in enumerate(pairs)]
    for load in loads:
        load.start()

    def remote(src, dst, send, recv, who):
        copy = pltpu.make_async_remote_copy(
            src_ref=src, dst_ref=dst, send_sem=send, recv_sem=recv, device_id=who, device_id_type=MESH
        )
        copy.start()
        return copy

    sent = []

    def scatter(phase, src, dst):
        return [
            remote(src(f_peer(k)), dst(k), f_send.at[phase, k], f_recv.at[phase, k], (f_peer(k), d))
            for k in range(1, nf)
        ]

    def block(g, kk, k):
        who = chip_from(kk)
        if g == 1:
            return pair0.at[who, :, tile(f_from(k), acts), :]
        if g == 0:
            who = core * chips + who
        at = pl.ds(pl.multiple_of(who * rows + f_from(k) * acts, acts), acts)
        return (every if g == 0 else pair1).at[at, :]

    across, to_core, along = {}, {}, {}

    def keep_copy(table, key, copy):
        table[key] = copy
        sent.append(copy)

    def share(g, kk):
        mine = block(g, kk, 0)
        for k in range(1, nf):
            keep_copy(across, (g, kk, k), remote(
                mine, mine, x_send.at[g, kk, k], x_recv.at[g, kk, k], (f_peer(k), d)
            ))

    def begin(g):
        mine = block(g, 0, 0)
        for k in range(1, chips):
            keep_copy(along, (g, k), remote(
                mine, mine, z_send.at[g, k], z_recv.at[g, k], (f, d_peer(k))
            ))
        share(g, 0)

    def from_z(g):
        for kk in range(1, chips):
            along[g, kk].wait_recv()
            share(g, kk)

    def from_f(g, kk):
        for k in range(1, nf):
            across[g, kk, k].wait_recv()

    def swap(g, kk):
        at = tile(core * chips + chip_from(kk), rows)
        mine = every.at[at, :] if g == 0 else seconds.at[g - 1, at, :]
        keep_copy(to_core, (g, kk), remote(
            mine, mine, c_send.at[g, kk], c_recv.at[g, kk], (f, sibling)
        ))

    def swapped(g):
        for kk in range(chips):
            to_core[g, kk].wait_recv()

    for load in loads[:4]:
        load.wait()
    normed, left = attend(noise, action, kv, flow)
    resid[...] = left
    own = pl.ds(pl.multiple_of((core * chips + chip) * rows + f * acts, acts), acts)
    every[own, :] = normed
    lane = lax.broadcasted_iota(jnp.int32, (acts, acts), 1)
    line = lax.broadcasted_iota(jnp.int32, (acts, acts), 0)
    valid = jnp.sum(
        jnp.where(lane == line, jnp.broadcast_to(mask[...].astype(F32), (acts, acts)), 0.0), -1, keepdims=True
    )
    pl.semaphore_wait(barrier, nf - 1 + chips)
    begin(0)
    group_at = tile(chip, rows)

    def first(whole, at, cut):
        group = every[whole, :]
        pre = dot32(group, w_up[:, cut])
        tangent = dot32(group, gradb[:, cut])
        sig = 1.0 / (1.0 + jnp.exp(-pre))
        slope = sig * (1.0 + pre * (1.0 - sig))
        slopes[at, cut] = slope
        curves[at, cut] = sig * (1.0 - sig) * (2.0 + pre * (1.0 - 2.0 * sig))
        tan0[at, cut] = tangent
        return pre * sig, slope * tangent

    def first_own(i):
        cut = tile(i, step)
        active, linear = first(tile(core * chips + chip, rows), group_at, cut)
        lhs[0:rows, cut] = active.astype(BF)
        lhs[rows : 2 * rows, cut] = linear.astype(BF)

    loads[5].wait()

    def narrow(i):
        cut = tile(i, wide)
        gradb[cut, :] = grad[cut, :].astype(BF)

    loop(width // wide, narrow)
    loads[4].wait()
    from_f(0, 0)
    swap(0, 0)
    first_own(0)
    from_z(0)
    if hid > step:
        pl.loop(1, hid // step)(first_own)
    loads[6].wait()

    def down(i):
        cut = tile(i, wide)
        part[:, cut] = dot32(lhs[...], w_down[:, cut]).astype(BF)

    loop(width // wide, down)

    def rows_of(p, q):
        return pl.ds(pl.multiple_of(q * rows + p * acts, acts), acts)

    outs = scatter(0, lambda p: part.at[rows_of(p, 0), :], lambda k: land0.at[k, 0:acts, :])
    moves = scatter(1, lambda p: part.at[rows_of(p, 1), :], lambda k: land0.at[k, acts : 2 * acts, :])

    def summed(copies, q, land, lo):
        value = part[rows_of(f, q), :].astype(F32)
        for k in range(1, nf):
            copies[k - 1].wait_recv()
            value = value + land[k, lo : lo + acts, :].astype(F32)
        return value

    here = tile(f, acts)
    pair0[chip, 0, here, :] = (valid * (resid[...] + summed(outs, 0, land0, 0))).astype(BF)
    pair0[chip, 1, here, :] = (valid * summed(moves, 1, land0, acts)).astype(BF)
    begin(1)
    for kk in range(1, chips):
        from_f(0, kk)
        swap(0, kk)

    def rest(i):
        first(tile(core, pack), slice(None), tile(i, step))

    rest(0)
    from_z(1)
    if hid > step:
        pl.loop(1, hid // step)(rest)
    swapped(0)

    def grams(i):
        cut = tile(i, pack)
        gram[:, cut] = (dot_t(every[tile(core, pack), :], every[cut, :]) * (1.0 / total)).astype(BF)

    loop(CORES, grams)

    def flip(i):
        cut = tile(i, wide)
        flipped[cut, :] = every[:, cut].T

    loop(width // wide, flip)

    def bend(kk):
        at = tile(chip_from(kk), rows)
        whole = tile(core * chips + chip_from(kk), rows)

        def body(i):
            cut = tile(i, step)
            both = dot_t(pair0[chip_from(kk)].reshape(2 * rows, width), w_down[cut, :])
            pull = both[0:rows]
            pulled[at, cut] = pull
            seconds[0, whole, cut] = (
                both[rows : 2 * rows] * slopes[at, cut] + pull * curves[at, cut] * tan0[at, cut]
            ).astype(BF)

        loop(hid // step, body)

    for kk in range(chips):
        from_f(1, kk)
        bend(kk)
        swap(1, kk)
    swapped(1)

    def again(at, cut):
        tangent = (1.0 + keep) * tan0[at, cut] - dot32(gram[at, :], seconds[0, :, cut])
        tan1[at, cut] = tangent
        return tangent

    def again_own(i):
        cut = tile(i, step)
        lhs[0:rows, cut] = (slopes[group_at, cut] * again(group_at, cut)).astype(BF)

    loop(hid // step, again_own)
    for copy in outs + moves:
        copy.wait_send()

    def down_again(i):
        cut = tile(i, wide)
        part[0:rows, cut] = dot32(lhs[0:rows, :], w_down[:, cut]).astype(BF)

    loop(width // wide, down_again)
    moves1 = scatter(2, lambda p: part.at[rows_of(p, 0), :], lambda k: land1.at[k])
    sent.extend(moves1)

    def again_all(i):
        again(slice(None), tile(i, step))

    loop(hid // step, again_all)
    pair1[pl.ds(pl.multiple_of(chip * rows + f * acts, acts), acts), :] = (valid * summed(moves1, 0, land1, 0)).astype(BF)
    begin(2)

    def settle(i):
        cut = tile(i, wide)
        change = dot32(flipped[cut, :], seconds[0])
        grad[cut, :] = (1.0 + keep + keep * keep) * grad[cut, :] - (keep / total) * change

    half = max(1, width // wide // 2)
    pl.loop(0, half)(settle)
    from_z(2)
    pl.loop(half, width // wide)(settle)

    def bend_again(kk):
        at = tile(chip_from(kk), rows)
        whole = tile(core * chips + chip_from(kk), rows)

        def body(i):
            cut = tile(i, step)
            both = dot_t(pair1[at, :], w_down[cut, :])
            seconds[1, whole, cut] = (
                both * slopes[at, cut] + pulled[at, cut] * curves[at, cut] * tan1[at, cut]
            ).astype(BF)

        loop(hid // step, body)

    for kk in range(chips):
        from_f(2, kk)
        bend_again(kk)
        swap(2, kk)
    swapped(2)

    def rate(i, terms):
        cut = tile(i, step)
        projected = tan0[group_at, cut] + keep * tan1[group_at, cut]
        projected = projected - dot32(gram[group_at, :], seconds[1, :, cut])
        return terms + projected * (pulled[group_at, cut] * slopes[group_at, cut])

    terms = lax.fori_loop(0, hid // step, rate, jnp.zeros((rows, step), F32))
    for p in range(nf):
        one = jnp.sum(terms[p * acts : (p + 1) * acts], 0, keepdims=True)
        tally[p] = jnp.broadcast_to(jnp.sum(one, -1, keepdims=True), tally.shape[1:])
    votes = scatter(3, lambda p: tally.at[p], lambda k: tally_in.at[k])
    sent.extend(votes)
    stores = []
    for i in range(width // wide):
        cut = pl.ds(i * wide, wide)
        grad[cut, :] = grad[cut, :] - dot32(flipped[cut, :], seconds[1]) * (1.0 / total)
        stores.append(pltpu.make_async_copy(grad.at[cut, :], out.at[cut, :], store_sem.at[i]))
        stores[-1].start()
    value = tally[f]
    for k in range(1, nf):
        votes[k - 1].wait_recv()
        value = value + tally_in[k]
    score[...] = -value / (acts * math.sqrt(width * hid * nf))
    for copy in sent:
        copy.wait_send()
    for store in stores:
        store.wait()


def spread_call(nf, nd, noise, action, kv, flow, mask, w_up, w_down, grad):
    acts, width = noise.shape
    hid = w_up.shape[1]
    rows = nf * acts
    total = nd * rows
    chips = nd // CORES
    vmem = pl.BlockSpec(memory_space=pltpu.VMEM)
    anywhere = pl.BlockSpec(memory_space=pl.ANY)
    dma = pltpu.SemaphoreType.DMA
    half, full = (lambda *s: pltpu.VMEM(s, BF)), (lambda *s: pltpu.VMEM(s, F32))
    vector, score = pl.pallas_call(
        functools.partial(spread, nf, nd),
        out_shape=(jax.ShapeDtypeStruct((width, hid), F32), jax.ShapeDtypeStruct((8, 128), F32)),
        in_specs=[anywhere] * 3 + [pl.BlockSpec(memory_space=pltpu.SMEM)] + [anywhere] * 4,
        out_specs=(anywhere, vmem),
        scratch_shapes=[
            half(acts, width), half(acts, width), half(*kv.shape), pltpu.VMEM((1, acts), jnp.int32),
            half(width, hid), half(hid, width), full(width, hid), half(width, hid),
            half(total, width), half(width, total), half(2, total, hid), half(total // CORES, total),
        ] + [full(total // CORES, hid)] * 5 + [
            half(2 * rows, hid), half(2 * rows, width), half(nf, 2 * acts, width), half(nf, acts, width),
            half(chips, 2, rows, width), half(total // CORES, width),
            full(acts, width), full(nf, 8, 128), full(nf, 8, 128),
            dma((7,)), dma((max(1, width // 256),)), dma((4, nf)), dma((4, nf)),
            dma((3, chips)), dma((3, chips)), dma((3, chips, nf)), dma((3, chips, nf)),
            dma((3, chips)), dma((3, chips)),
        ],
        compiler_params=pltpu.CompilerParams(
            collective_id=0, has_side_effects=True, vmem_limit_bytes=44 * 1024 * 1024
        ),
        name="lissa",
    )(noise, action, kv, flow, mask.reshape(1, acts), w_up, w_down, grad)
    return vector, score[0, 0:1]


def finish(total, every, mix, grad, out):
    change = lax.dot_general(
        every[...], mix[...], (((0,), (0,)), ((), ())), preferred_element_type=F32
    )
    out[...] = (1.0 + keep + keep * keep) * grad[...] - change / total


def shards(nf, nd, noise, action, kv, flow, mask, w_up, w_down, grad):
    acts, width = noise.shape
    hid = w_up.shape[1]
    rows = nf * acts
    total = nd * rows
    if total <= 512:
        return spread_call(nf, nd, noise, action, kv, flow, mask, w_up, w_down, grad)
    vmem = pl.BlockSpec(memory_space=pltpu.VMEM)
    anywhere = pl.BlockSpec(memory_space=pl.ANY)
    dma = pltpu.SemaphoreType.DMA
    chips = nd // CORES
    every, mix, score = pl.pallas_call(
        functools.partial(kernel, nf, nd),
        out_shape=(
            jax.ShapeDtypeStruct((total, width), BF),
            jax.ShapeDtypeStruct((total, hid), BF),
            jax.ShapeDtypeStruct((8, 128), F32),
        ),
        in_specs=[
            vmem, vmem, vmem, pl.BlockSpec(memory_space=pltpu.SMEM), vmem, anywhere, anywhere, anywhere,
        ],
        out_specs=(anywhere, anywhere, vmem),
        scratch_shapes=[
            pltpu.VMEM((width, hid), BF),
            pltpu.VMEM((hid, width), BF),
            pltpu.VMEM((width, hid), F32),
            pltpu.VMEM((total, width), BF),
            pltpu.VMEM((total, hid), BF),
            pltpu.VMEM((total, hid), BF),
            pltpu.VMEM((rows, total), BF),
            pltpu.VMEM((rows, hid), F32),
            pltpu.VMEM((rows, hid), F32),
            pltpu.VMEM((rows, hid), F32),
            pltpu.VMEM((rows, hid), F32),
            pltpu.VMEM((rows, hid), F32),
            pltpu.VMEM((2 * rows, hid), BF),
            pltpu.VMEM((2 * rows, width), BF),
            pltpu.VMEM((nf, 2 * acts, width), BF),
            pltpu.VMEM((nf, acts, width), BF),
            pltpu.VMEM((2 * rows, width), BF),
            pltpu.VMEM((rows, width), BF),
            pltpu.VMEM((acts, width), F32),
            pltpu.VMEM((nf, 8, 128), F32),
            pltpu.VMEM((nf, 8, 128), F32),
            dma((3,)),
            dma((2,)),
            dma((8, nf)),
            dma((8, nf)),
            dma((3, chips)),
            dma((3, chips)),
            dma((3, chips)),
            dma((3, chips)),
        ],
        compiler_params=pltpu.CompilerParams(
            collective_id=0, has_side_effects=True, vmem_limit_bytes=52 * 1024 * 1024
        ),
        name="lissa",
    )(noise, action, kv, flow, mask.reshape(1, acts), w_up, w_down, grad)
    strip = 128
    vector = pl.pallas_call(
        functools.partial(finish, total),
        out_shape=jax.ShapeDtypeStruct((width, hid), F32),
        grid=(width // strip,),
        in_specs=[
            pl.BlockSpec((total, strip), lambda i: (0, i)),
            pl.BlockSpec((total, hid), lambda i: (0, 0)),
            pl.BlockSpec((strip, hid), lambda i: (i, 0)),
        ],
        out_specs=pl.BlockSpec((strip, hid), lambda i: (i, 0)),
        compiler_params=pltpu.CompilerParams(vmem_limit_bytes=40 * 1024 * 1024),
        name="finish",
    )(every, mix, grad)
    return vector, score[0, 0:1]


def solution(mesh):
    placed = (
        P(("fsdp", "dp"), None),
        P(("fsdp", "dp"), None),
        P(None, ("fsdp", "dp"), None, None),
        P(("fsdp", "dp")),
        P(("fsdp", "dp")),
        P(None, "fsdp"),
        P("fsdp", None),
        P(None, "fsdp"),
    )
    return jax.shard_map(
        functools.partial(shards, mesh.shape["fsdp"], mesh.shape["dp"]),
        mesh=mesh,
        in_specs=placed,
        out_specs=(P(None, "fsdp"), P(("fsdp", "dp"))),
        check_vma=False,
    )
```

```python
import functools
import math

import jax
import jax.numpy as jnp
from jax import lax
from jax.experimental import pallas as pl
from jax.experimental.pallas import tpu as pltpu
from jax.sharding import PartitionSpec as P

STEPS_T = 10
CORES = 2

epsilon = 1e-06
sharpness_divisor = 6.0
keep = 1.0 - 0.01

BF = jnp.bfloat16
F32 = jnp.float32
MESH = pl.DeviceIdType.MESH


def dot32(a, b):
    return jnp.dot(a, b, preferred_element_type=F32)


def dot_t(a, b):
    return lax.dot_general(a, b, (((1,), (1,)), ((), ())), preferred_element_type=F32)


def loop(count, body):
    if count == 1:
        body(0)
    else:
        pl.loop(0, count)(body)


def tile(i, size):
    return pl.ds(pl.multiple_of(i * size, size), size)


def attend(noise, action, kv, flow):
    acts, width = noise.shape
    span = kv.shape[3]
    heads = width // span
    time = (flow[0].astype(F32) + 1.0) / (STEPS_T + 1.0)
    noisy = noise[...].astype(F32)
    clean = action[...].astype(F32)
    inputs = time * noisy + (1.0 - time) * clean
    queries = jnp.concatenate([inputs[:, h * span : (h + 1) * span] for h in range(heads)], 0)
    queries = queries * lax.rsqrt(jnp.mean(queries * queries, -1, keepdims=True) + epsilon)
    keys = kv[0, 0].astype(F32)
    keys = keys * lax.rsqrt(jnp.mean(keys * keys, -1, keepdims=True) + epsilon)
    expo = jnp.exp(dot_t(queries.astype(BF), keys.astype(BF)) * (sharpness_divisor / span))
    weights = (expo / jnp.sum(expo, -1, keepdims=True)).astype(BF)
    mixed = dot32(weights, kv[1, 0])
    mixed = jnp.concatenate([mixed[h * acts : (h + 1) * acts] for h in range(heads)], 1)
    hidden = inputs + mixed
    normed = hidden * lax.rsqrt(jnp.mean(hidden * hidden, -1, keepdims=True) + epsilon)
    return normed.astype(BF), hidden - (noisy - clean)


def kernel(
    nf, nd,
    noise, action, kv, flow, mask, w_up_h, w_down_h, grad_h,
    every_o, mix_o, score,
    w_up, w_down, grad, every, seconds0, seconds1, gram,
    slopes, curves, pulled, tan0, tan1, lhs, part, land0, land1, pair0, pair1,
    resid, tally, tally_in,
    load_sem, store_sem, f_send, f_recv, z_send, z_recv, c_send, c_recv,
):
    acts, width = noise.shape
    hid = w_up.shape[1]
    rows = nf * acts
    total = nd * rows
    chips = nd // CORES
    f = lax.axis_index("fsdp")
    d = lax.axis_index("dp")
    chip, core = d // CORES, d % CORES
    sibling = chip * CORES + (1 - core)

    def f_peer(k):
        return lax.rem(f + k, nf)

    def d_peer(k):
        return lax.rem(chip + k, chips) * CORES + core

    def d_from(k):
        return lax.rem(chip + chips - k, chips) * CORES + core

    barrier = pltpu.get_barrier_semaphore()
    for k in range(1, nf):
        pl.semaphore_signal(barrier, inc=1, device_id=(f_peer(k), d), device_id_type=MESH)
    for k in range(1, chips):
        pl.semaphore_signal(barrier, inc=1, device_id=(f, d_peer(k)), device_id_type=MESH)
    pl.semaphore_signal(barrier, inc=1, device_id=(f, sibling), device_id_type=MESH)

    loads = [
        pltpu.make_async_copy(src, dst, load_sem.at[i])
        for i, (src, dst) in enumerate(((w_up_h, w_up), (grad_h, grad), (w_down_h, w_down)))
    ]
    for load in loads:
        load.start()

    def remote(src, dst, send, recv, who):
        copy = pltpu.make_async_remote_copy(
            src_ref=src, dst_ref=dst, send_sem=send, recv_sem=recv, device_id=who, device_id_type=MESH
        )
        copy.start()
        return copy

    sent = []

    def fsdp(phase, src, dst):
        copies = [
            remote(src(f_peer(k)), dst(k), f_send.at[phase, k], f_recv.at[phase, k], (f_peer(k), d))
            for k in range(1, nf)
        ]
        if phase not in (1, 2):
            sent.extend(copies)
        return copies

    def landed(copies):
        for copy in copies:
            copy.wait_recv()

    def dp_start(phase, buf):
        mine = buf.at[tile(d, rows), :]
        z = [
            remote(mine, mine, z_send.at[phase, k], z_recv.at[phase, k], (f, d_peer(k)))
            for k in range(1, chips)
        ]
        c = [remote(mine, mine, c_send.at[phase, 0], c_recv.at[phase, 0], (f, sibling))]
        sent.extend(z)
        sent.extend(c)
        return z, c

    def dp_forward(phase, buf, z, c):
        for k in range(1, chips):
            z[k - 1].wait_recv()
            block = buf.at[tile(d_from(k), rows), :]
            copy = remote(block, block, c_send.at[phase, k], c_recv.at[phase, k], (f, sibling))
            sent.append(copy)
            c.append(copy)

    normed, left = attend(noise, action, kv, flow)
    resid[...] = left
    own = pl.ds(pl.multiple_of(d * rows + f * acts, acts), acts)
    every[own, :] = normed
    lane = lax.broadcasted_iota(jnp.int32, (acts, acts), 1)
    line = lax.broadcasted_iota(jnp.int32, (acts, acts), 0)
    valid = jnp.sum(
        jnp.where(lane == line, jnp.broadcast_to(mask[...].astype(F32), (acts, acts)), 0.0), -1, keepdims=True
    )
    pl.semaphore_wait(barrier, nf - 1 + chips)

    mine = every.at[own, :]
    landed(fsdp(0, lambda p: mine, lambda k: mine))
    group_at = tile(d, rows)
    z_n, c_n = dp_start(0, every)

    loads[0].wait()
    loads[1].wait()
    step = min(256, hid)

    def first(i):
        cut = tile(i, step)
        group = every[group_at, :]
        pre = dot32(group, w_up[:, cut])
        tangent = dot32(group, grad[:, cut].astype(BF))
        sig = 1.0 / (1.0 + jnp.exp(-pre))
        slope = sig * (1.0 + pre * (1.0 - sig))
        slopes[:, cut] = slope
        curves[:, cut] = sig * (1.0 - sig) * (2.0 + pre * (1.0 - 2.0 * sig))
        tan0[:, cut] = tangent
        lhs[0:rows, cut] = (pre * sig).astype(BF)
        lhs[rows : 2 * rows, cut] = (slope * tangent).astype(BF)

    loop(hid // step, first)
    loads[2].wait()
    wide = min(256, width)

    def down(i):
        cut = tile(i, wide)
        part[:, cut] = dot32(lhs[...], w_down[:, cut]).astype(BF)

    loop(width // wide, down)

    def rows_of(p, q):
        return pl.ds(pl.multiple_of(q * rows + p * acts, acts), acts)

    outs = fsdp(1, lambda p: part.at[rows_of(p, 0), :], lambda k: land0.at[k, 0:acts, :])
    moves = fsdp(2, lambda p: part.at[rows_of(p, 1), :], lambda k: land0.at[k, acts : 2 * acts, :])

    def summed(copies, q, land, lo):
        value = part[rows_of(f, q), :].astype(F32)
        for k in range(1, nf):
            copies[k - 1].wait_recv()
            value = value + land[k, lo : lo + acts, :].astype(F32)
        return value

    err = (valid * (resid[...] + summed(outs, 0, land0, 0))).astype(BF)
    pair0[rows_of(f, 0), :] = err
    errs = fsdp(3, lambda p: pair0.at[rows_of(f, 0), :], lambda k: pair0.at[rows_of(f, 0), :])
    pair0[rows_of(f, 1), :] = (valid * summed(moves, 1, land0, acts)).astype(BF)
    merrs = fsdp(4, lambda p: pair0.at[rows_of(f, 1), :], lambda k: pair0.at[rows_of(f, 1), :])
    dp_forward(0, every, z_n, c_n)
    landed(errs)
    landed(merrs)

    def bend(i):
        cut = tile(i, step)
        both = dot_t(pair0[...], w_down[cut, :])
        pull = both[0:rows]
        pulled[:, cut] = pull
        seconds0[group_at, cut] = (
            both[rows : 2 * rows] * slopes[:, cut] + pull * curves[:, cut] * tan0[:, cut]
        ).astype(BF)

    loop(hid // step, bend)
    z_0, c_0 = dp_start(1, seconds0)
    landed(c_n)
    keep_every = pltpu.make_async_copy(every, every_o, store_sem.at[0])
    keep_every.start()
    chunk = min(512, total)

    def grams(i):
        cut = tile(i, chunk)
        gram[:, cut] = (dot_t(every[group_at, :], every[cut, :]) / total).astype(BF)

    loop(total // chunk, grams)
    dp_forward(1, seconds0, z_0, c_0)
    landed(c_0)

    def fold(seconds, cut):
        if total == chunk:
            return dot32(gram[...], seconds[:, cut])
        return lax.fori_loop(
            0,
            total // chunk,
            lambda j, v: v + dot32(gram[:, tile(j, chunk)], seconds[tile(j, chunk), cut]),
            jnp.zeros((rows, step), F32),
        )

    def again(i):
        cut = tile(i, step)
        tangent = (1.0 + keep) * tan0[:, cut] - fold(seconds0, cut)
        tan1[:, cut] = tangent
        lhs[0:rows, cut] = (slopes[:, cut] * tangent).astype(BF)

    loop(hid // step, again)
    for copy in outs + moves:
        copy.wait_send()

    def down_again(i):
        cut = tile(i, wide)
        part[0:rows, cut] = dot32(lhs[0:rows, :], w_down[:, cut]).astype(BF)

    loop(width // wide, down_again)
    moves1 = fsdp(5, lambda p: part.at[rows_of(p, 0), :], lambda k: land1.at[k])
    pair1[rows_of(f, 0), :] = (valid * summed(moves1, 0, land1, 0)).astype(BF)
    landed(fsdp(6, lambda p: pair1.at[rows_of(f, 0), :], lambda k: pair1.at[rows_of(f, 0), :]))

    def bend_again(i):
        cut = tile(i, step)
        both = dot_t(pair1[...], w_down[cut, :])
        seconds1[group_at, cut] = (
            both * slopes[:, cut] + pulled[:, cut] * curves[:, cut] * tan1[:, cut]
        ).astype(BF)

    loop(hid // step, bend_again)
    z_1, c_1 = dp_start(2, seconds1)
    dp_forward(2, seconds1, z_1, c_1)
    landed(c_1)
    for copy in sent:
        copy.wait_send()

    def blend(i):
        cut = tile(i, rows)
        seconds1[cut, :] = (
            keep * seconds0[cut, :].astype(F32) + seconds1[cut, :].astype(F32)
        ).astype(BF)

    loop(nd, blend)
    keep_mix = pltpu.make_async_copy(seconds1, mix_o, store_sem.at[1])
    keep_mix.start()
    scale = 1.0 + keep + keep * keep

    def rate(i, terms):
        cut = tile(i, step)
        projected = scale * tan0[:, cut] - fold(seconds1, cut)
        return terms + projected * (pulled[:, cut] * slopes[:, cut])

    terms = lax.fori_loop(0, hid // step, rate, jnp.zeros((rows, step), F32))
    for p in range(nf):
        one = jnp.sum(terms[p * acts : (p + 1) * acts], 0, keepdims=True)
        tally[p] = jnp.broadcast_to(jnp.sum(one, -1, keepdims=True), tally.shape[1:])
    votes = [
        remote(tally.at[f_peer(k)], tally_in.at[k], f_send.at[7, k], f_recv.at[7, k], (f_peer(k), d))
        for k in range(1, nf)
    ]
    value = tally[f]
    for k in range(1, nf):
        votes[k - 1].wait_recv()
        value = value + tally_in[k]
    score[...] = -value / (acts * math.sqrt(width * hid * nf))
    for copy in votes:
        copy.wait_send()
    keep_every.wait()
    keep_mix.wait()


def spread(
    nf, nd,
    noise_h, action_h, kv_h, flow, mask_h, w_up_h, w_down_h, grad_h,
    out, score,
    noise, action, kv, mask, w_up, w_down, grad, gradb, every, flipped, seconds, gram,
    slopes, curves, pulled, tan0, tan1, lhs, part, land0, land1, pair0, pair1,
    resid, tally, tally_in,
    load_sem, store_sem, f_send, f_recv, z_send, z_recv, x_send, x_recv, c_send, c_recv,
):
    acts, width = noise.shape
    hid = w_up.shape[1]
    rows = nf * acts
    total = nd * rows
    chips = nd // CORES
    pack = chips * rows
    step = min(256, hid)
    wide = min(256, width)
    f = lax.axis_index("fsdp")
    d = lax.axis_index("dp")
    chip, core = d // CORES, d % CORES
    sibling = chip * CORES + (1 - core)

    def f_peer(k):
        return lax.rem(f + k, nf)

    def f_from(k):
        return lax.rem(f + nf - k, nf)

    def d_peer(k):
        return lax.rem(chip + k, chips) * CORES + core

    def chip_from(k):
        return lax.rem(chip + chips - k, chips)

    barrier = pltpu.get_barrier_semaphore()
    for k in range(1, nf):
        pl.semaphore_signal(barrier, inc=1, device_id=(f_peer(k), d), device_id_type=MESH)
    for k in range(1, chips):
        pl.semaphore_signal(barrier, inc=1, device_id=(f, d_peer(k)), device_id_type=MESH)
    pl.semaphore_signal(barrier, inc=1, device_id=(f, sibling), device_id_type=MESH)

    pairs = (
        (noise_h, noise), (action_h, action), (kv_h, kv), (mask_h, mask),
        (w_up_h, w_up), (grad_h, grad), (w_down_h, w_down),
    )
    loads = [pltpu.make_async_copy(src, dst, load_sem.at[i]) for i, (src, dst) in enumerate(pairs)]
    for load in loads:
        load.start()

    def remote(src, dst, send, recv, who):
        copy = pltpu.make_async_remote_copy(
            src_ref=src, dst_ref=dst, send_sem=send, recv_sem=recv, device_id=who, device_id_type=MESH
        )
        copy.start()
        return copy

    sent = []

    def scatter(phase, src, dst):
        return [
            remote(src(f_peer(k)), dst(k), f_send.at[phase, k], f_recv.at[phase, k], (f_peer(k), d))
            for k in range(1, nf)
        ]

    def block(g, kk, k):
        who = chip_from(kk)
        if g == 1:
            return pair0.at[who, :, tile(f_from(k), acts), :]
        if g == 0:
            who = core * chips + who
        at = pl.ds(pl.multiple_of(who * rows + f_from(k) * acts, acts), acts)
        return (every if g == 0 else pair1).at[at, :]

    across, to_core, along = {}, {}, {}

    def keep_copy(table, key, copy):
        table[key] = copy
        sent.append(copy)

    def share(g, kk):
        mine = block(g, kk, 0)
        for k in range(1, nf):
            keep_copy(across, (g, kk, k), remote(
                mine, mine, x_send.at[g, kk, k], x_recv.at[g, kk, k], (f_peer(k), d)
            ))

    def begin(g):
        mine = block(g, 0, 0)
        for k in range(1, chips):
            keep_copy(along, (g, k), remote(
                mine, mine, z_send.at[g, k], z_recv.at[g, k], (f, d_peer(k))
            ))
        share(g, 0)

    def from_z(g):
        for kk in range(1, chips):
            along[g, kk].wait_recv()
            share(g, kk)

    def from_f(g, kk):
        for k in range(1, nf):
            across[g, kk, k].wait_recv()

    def swap(g, kk):
        at = tile(core * chips + chip_from(kk), rows)
        mine = every.at[at, :] if g == 0 else seconds.at[g - 1, at, :]
        keep_copy(to_core, (g, kk), remote(
            mine, mine, c_send.at[g, kk], c_recv.at[g, kk], (f, sibling)
        ))

    def swapped(g):
        for kk in range(chips):
            to_core[g, kk].wait_recv()

    for load in loads[:4]:
        load.wait()
    normed, left = attend(noise, action, kv, flow)
    resid[...] = left
    own = pl.ds(pl.multiple_of((core * chips + chip) * rows + f * acts, acts), acts)
    every[own, :] = normed
    lane = lax.broadcasted_iota(jnp.int32, (acts, acts), 1)
    line = lax.broadcasted_iota(jnp.int32, (acts, acts), 0)
    valid = jnp.sum(
        jnp.where(lane == line, jnp.broadcast_to(mask[...].astype(F32), (acts, acts)), 0.0), -1, keepdims=True
    )
    pl.semaphore_wait(barrier, nf - 1 + chips)
    begin(0)
    group_at = tile(chip, rows)

    def first(whole, at, cut):
        group = every[whole, :]
        pre = dot32(group, w_up[:, cut])
        tangent = dot32(group, gradb[:, cut])
        sig = 1.0 / (1.0 + jnp.exp(-pre))
        slope = sig * (1.0 + pre * (1.0 - sig))
        slopes[at, cut] = slope
        curves[at, cut] = sig * (1.0 - sig) * (2.0 + pre * (1.0 - 2.0 * sig))
        tan0[at, cut] = tangent
        return pre * sig, slope * tangent

    def first_own(i):
        cut = tile(i, step)
        active, linear = first(tile(core * chips + chip, rows), group_at, cut)
        lhs[0:rows, cut] = active.astype(BF)
        lhs[rows : 2 * rows, cut] = linear.astype(BF)

    loads[5].wait()

    def narrow(i):
        cut = tile(i, wide)
        gradb[cut, :] = grad[cut, :].astype(BF)

    loop(width // wide, narrow)
    loads[4].wait()
    from_f(0, 0)
    swap(0, 0)
    first_own(0)
    from_z(0)
    if hid > step:
        pl.loop(1, hid // step)(first_own)
    loads[6].wait()

    def down(i):
        cut = tile(i, wide)
        part[:, cut] = dot32(lhs[...], w_down[:, cut]).astype(BF)

    loop(width // wide, down)

    def rows_of(p, q):
        return pl.ds(pl.multiple_of(q * rows + p * acts, acts), acts)

    outs = scatter(0, lambda p: part.at[rows_of(p, 0), :], lambda k: land0.at[k, 0:acts, :])
    moves = scatter(1, lambda p: part.at[rows_of(p, 1), :], lambda k: land0.at[k, acts : 2 * acts, :])

    def summed(copies, q, land, lo):
        value = part[rows_of(f, q), :].astype(F32)
        for k in range(1, nf):
            copies[k - 1].wait_recv()
            value = value + land[k, lo : lo + acts, :].astype(F32)
        return value

    here = tile(f, acts)
    pair0[chip, 0, here, :] = (valid * (resid[...] + summed(outs, 0, land0, 0))).astype(BF)
    pair0[chip, 1, here, :] = (valid * summed(moves, 1, land0, acts)).astype(BF)
    begin(1)
    for kk in range(1, chips):
        from_f(0, kk)
        swap(0, kk)

    def rest(i):
        first(tile(core, pack), slice(None), tile(i, step))

    rest(0)
    from_z(1)
    if hid > step:
        pl.loop(1, hid // step)(rest)
    swapped(0)

    def grams(i):
        cut = tile(i, pack)
        gram[:, cut] = (dot_t(every[tile(core, pack), :], every[cut, :]) * (1.0 / total)).astype(BF)

    loop(CORES, grams)

    def flip(i):
        cut = tile(i, wide)
        flipped[cut, :] = every[:, cut].T

    loop(width // wide, flip)

    def bend(kk):
        at = tile(chip_from(kk), rows)
        whole = tile(core * chips + chip_from(kk), rows)

        def body(i):
            cut = tile(i, step)
            both = dot_t(pair0[chip_from(kk)].reshape(2 * rows, width), w_down[cut, :])
            pull = both[0:rows]
            pulled[at, cut] = pull
            seconds[0, whole, cut] = (
                both[rows : 2 * rows] * slopes[at, cut] + pull * curves[at, cut] * tan0[at, cut]
            ).astype(BF)

        loop(hid // step, body)

    for kk in range(chips):
        from_f(1, kk)
        bend(kk)
        swap(1, kk)
    swapped(1)

    def again(at, cut):
        tangent = (1.0 + keep) * tan0[at, cut] - dot32(gram[at, :], seconds[0, :, cut])
        tan1[at, cut] = tangent
        return tangent

    def again_own(i):
        cut = tile(i, step)
        lhs[0:rows, cut] = (slopes[group_at, cut] * again(group_at, cut)).astype(BF)

    loop(hid // step, again_own)
    for copy in outs + moves:
        copy.wait_send()

    def down_again(i):
        cut = tile(i, wide)
        part[0:rows, cut] = dot32(lhs[0:rows, :], w_down[:, cut]).astype(BF)

    loop(width // wide, down_again)
    moves1 = scatter(2, lambda p: part.at[rows_of(p, 0), :], lambda k: land1.at[k])
    sent.extend(moves1)

    def again_all(i):
        again(slice(None), tile(i, step))

    loop(hid // step, again_all)
    pair1[pl.ds(pl.multiple_of(chip * rows + f * acts, acts), acts), :] = (valid * summed(moves1, 0, land1, 0)).astype(BF)
    begin(2)

    def settle(i):
        cut = tile(i, wide)
        change = dot32(flipped[cut, :], seconds[0])
        grad[cut, :] = (1.0 + keep + keep * keep) * grad[cut, :] - (keep / total) * change

    half = max(1, width // wide // 2)
    pl.loop(0, half)(settle)
    from_z(2)
    pl.loop(half, width // wide)(settle)

    def bend_again(kk):
        at = tile(chip_from(kk), rows)
        whole = tile(core * chips + chip_from(kk), rows)

        def body(i):
            cut = tile(i, step)
            both = dot_t(pair1[at, :], w_down[cut, :])
            seconds[1, whole, cut] = (
                both * slopes[at, cut] + pulled[at, cut] * curves[at, cut] * tan1[at, cut]
            ).astype(BF)

        loop(hid // step, body)

    for kk in range(chips):
        from_f(2, kk)
        bend_again(kk)
        swap(2, kk)
    swapped(2)

    def rate(i, terms):
        cut = tile(i, step)
        projected = tan0[group_at, cut] + keep * tan1[group_at, cut]
        projected = projected - dot32(gram[group_at, :], seconds[1, :, cut])
        return terms + projected * (pulled[group_at, cut] * slopes[group_at, cut])

    terms = lax.fori_loop(0, hid // step, rate, jnp.zeros((rows, step), F32))
    for p in range(nf):
        one = jnp.sum(terms[p * acts : (p + 1) * acts], 0, keepdims=True)
        tally[p] = jnp.broadcast_to(jnp.sum(one, -1, keepdims=True), tally.shape[1:])
    votes = scatter(3, lambda p: tally.at[p], lambda k: tally_in.at[k])
    sent.extend(votes)
    stores = []
    for i in range(width // wide):
        cut = pl.ds(i * wide, wide)
        gradb[cut, :] = (grad[cut, :] - dot32(flipped[cut, :], seconds[1]) * (1.0 / total)).astype(BF)
        stores.append(pltpu.make_async_copy(gradb.at[cut, :], out.at[cut, :], store_sem.at[i]))
        stores[-1].start()
    value = tally[f]
    for k in range(1, nf):
        votes[k - 1].wait_recv()
        value = value + tally_in[k]
    score[...] = -value / (acts * math.sqrt(width * hid * nf))
    for copy in sent:
        copy.wait_send()
    for store in stores:
        store.wait()


def hand_out(held, tally, out, score, taken, stage, sems):
    parts = sems.shape[1]
    high = out.shape[0] // parts

    def move(i, to):
        at = pl.ds(i * high, high)
        src, dst = (stage, out) if to else (held, taken)
        return pltpu.make_async_copy(src.at[at, :], dst.at[at, :], sems.at[to, i])

    loads = [move(i, 0) for i in range(parts)]
    stores = [move(i, 1) for i in range(parts)]
    for load in loads:
        load.start()
    score[0] = tally[0, 0]
    for i, (load, store) in enumerate(zip(loads, stores)):
        load.wait()
        at = pl.ds(i * high, high)
        stage[at, :] = taken[at, :].astype(F32)
        store.start()
    for store in stores:
        store.wait()


def spread_call(nf, nd, noise, action, kv, flow, mask, w_up, w_down, grad):
    acts, width = noise.shape
    hid = w_up.shape[1]
    rows = nf * acts
    total = nd * rows
    chips = nd // CORES
    vmem = pl.BlockSpec(memory_space=pltpu.VMEM)
    anywhere = pl.BlockSpec(memory_space=pl.ANY)
    dma = pltpu.SemaphoreType.DMA
    half, full = (lambda *s: pltpu.VMEM(s, BF)), (lambda *s: pltpu.VMEM(s, F32))
    vector, score = pl.pallas_call(
        functools.partial(spread, nf, nd),
        out_shape=(jax.ShapeDtypeStruct((width, hid), BF), jax.ShapeDtypeStruct((8, 128), F32)),
        in_specs=[anywhere] * 3 + [pl.BlockSpec(memory_space=pltpu.SMEM)] + [anywhere] * 4,
        out_specs=(anywhere, vmem),
        scratch_shapes=[
            half(acts, width), half(acts, width), half(*kv.shape), pltpu.VMEM((1, acts), jnp.int32),
            half(width, hid), half(hid, width), full(width, hid), half(width, hid),
            half(total, width), half(width, total), half(2, total, hid), half(total // CORES, total),
        ] + [full(total // CORES, hid)] * 5 + [
            half(2 * rows, hid), half(2 * rows, width), half(nf, 2 * acts, width), half(nf, acts, width),
            half(chips, 2, rows, width), half(total // CORES, width),
            full(acts, width), full(nf, 8, 128), full(nf, 8, 128),
            dma((7,)), dma((max(1, width // 256),)), dma((4, nf)), dma((4, nf)),
            dma((3, chips)), dma((3, chips)), dma((3, chips, nf)), dma((3, chips, nf)),
            dma((3, chips)), dma((3, chips)),
        ],
        compiler_params=pltpu.CompilerParams(
            collective_id=0, has_side_effects=True, vmem_limit_bytes=60 * 1024 * 1024
        ),
        name="lissa",
    )(noise, action, kv, flow, mask.reshape(1, acts), w_up, w_down, grad)
    return pl.pallas_call(
        hand_out,
        out_shape=(jax.ShapeDtypeStruct((width, hid), F32), jax.ShapeDtypeStruct((1,), F32)),
        in_specs=[anywhere, vmem],
        out_specs=(anywhere, pl.BlockSpec(memory_space=pltpu.SMEM)),
        scratch_shapes=[half(width, hid), full(width, hid), dma((2, 8))],
        compiler_params=pltpu.CompilerParams(vmem_limit_bytes=60 * 1024 * 1024),
        name="hand_out",
    )(vector, score)


def finish(total, every, mix, grad, out):
    change = lax.dot_general(
        every[...], mix[...], (((0,), (0,)), ((), ())), preferred_element_type=F32
    )
    out[...] = (1.0 + keep + keep * keep) * grad[...] - change / total


def shards(nf, nd, noise, action, kv, flow, mask, w_up, w_down, grad):
    acts, width = noise.shape
    hid = w_up.shape[1]
    rows = nf * acts
    total = nd * rows
    if total <= 512:
        return spread_call(nf, nd, noise, action, kv, flow, mask, w_up, w_down, grad)
    vmem = pl.BlockSpec(memory_space=pltpu.VMEM)
    anywhere = pl.BlockSpec(memory_space=pl.ANY)
    dma = pltpu.SemaphoreType.DMA
    chips = nd // CORES
    every, mix, score = pl.pallas_call(
        functools.partial(kernel, nf, nd),
        out_shape=(
            jax.ShapeDtypeStruct((total, width), BF),
            jax.ShapeDtypeStruct((total, hid), BF),
            jax.ShapeDtypeStruct((8, 128), F32),
        ),
        in_specs=[
            vmem, vmem, vmem, pl.BlockSpec(memory_space=pltpu.SMEM), vmem, anywhere, anywhere, anywhere,
        ],
        out_specs=(anywhere, anywhere, vmem),
        scratch_shapes=[
            pltpu.VMEM((width, hid), BF),
            pltpu.VMEM((hid, width), BF),
            pltpu.VMEM((width, hid), F32),
            pltpu.VMEM((total, width), BF),
            pltpu.VMEM((total, hid), BF),
            pltpu.VMEM((total, hid), BF),
            pltpu.VMEM((rows, total), BF),
            pltpu.VMEM((rows, hid), F32),
            pltpu.VMEM((rows, hid), F32),
            pltpu.VMEM((rows, hid), F32),
            pltpu.VMEM((rows, hid), F32),
            pltpu.VMEM((rows, hid), F32),
            pltpu.VMEM((2 * rows, hid), BF),
            pltpu.VMEM((2 * rows, width), BF),
            pltpu.VMEM((nf, 2 * acts, width), BF),
            pltpu.VMEM((nf, acts, width), BF),
            pltpu.VMEM((2 * rows, width), BF),
            pltpu.VMEM((rows, width), BF),
            pltpu.VMEM((acts, width), F32),
            pltpu.VMEM((nf, 8, 128), F32),
            pltpu.VMEM((nf, 8, 128), F32),
            dma((3,)),
            dma((2,)),
            dma((8, nf)),
            dma((8, nf)),
            dma((3, chips)),
            dma((3, chips)),
            dma((3, chips)),
            dma((3, chips)),
        ],
        compiler_params=pltpu.CompilerParams(
            collective_id=0, has_side_effects=True, vmem_limit_bytes=52 * 1024 * 1024
        ),
        name="lissa",
    )(noise, action, kv, flow, mask.reshape(1, acts), w_up, w_down, grad)
    strip = 128
    vector = pl.pallas_call(
        functools.partial(finish, total),
        out_shape=jax.ShapeDtypeStruct((width, hid), F32),
        grid=(width // strip,),
        in_specs=[
            pl.BlockSpec((total, strip), lambda i: (0, i)),
            pl.BlockSpec((total, hid), lambda i: (0, 0)),
            pl.BlockSpec((strip, hid), lambda i: (i, 0)),
        ],
        out_specs=pl.BlockSpec((strip, hid), lambda i: (i, 0)),
        compiler_params=pltpu.CompilerParams(vmem_limit_bytes=40 * 1024 * 1024),
        name="finish",
    )(every, mix, grad)
    return vector, score[0, 0:1]


def solution(mesh):
    placed = (
        P(("fsdp", "dp"), None),
        P(("fsdp", "dp"), None),
        P(None, ("fsdp", "dp"), None, None),
        P(("fsdp", "dp")),
        P(("fsdp", "dp")),
        P(None, "fsdp"),
        P("fsdp", None),
        P(None, "fsdp"),
    )
    return jax.shard_map(
        functools.partial(shards, mesh.shape["fsdp"], mesh.shape["dp"]),
        mesh=mesh,
        in_specs=placed,
        out_specs=(P(None, "fsdp"), P(("fsdp", "dp"))),
        check_vma=False,
    )
```
